256 devices in a mesh: ctx: 32 (over y, z), tp: 8 (over x, core).
Axes of the slice: x: 4, y: 4, z: 8, core: 2. Of those that a mesh axis runs over, the one named last changes fastest.
Arguments:
- context_queries: bfloat16 [24576, 8192], P('ctx', 'tp'), may hold values from -9 to 9
- context_keys: bfloat16 [24576, 1024], P('ctx', 'tp'), may hold values from -4 to 4
- context_value_rows: bfloat16 [24576, 1024], P('ctx', 'tp'), may hold values from -6 to 6
- prompt_queries: bfloat16 [512, 8192], P('ctx', 'tp'), may hold values from -9 to 9
- prompt_key_rows: bfloat16 [512, 1024], P('ctx', 'tp'), may hold values from -4 to 4
- prompt_value_matrix: bfloat16 [512, 1024], P('ctx', 'tp'), may hold values from -6 to 6
- output_weight: bfloat16 [8192, 8192], P('tp', 'ctx'), may hold values from -0.0625 to 0.0625
Outputs:
- encoded: bfloat16 [24576, 8192], P('ctx', 'tp')
- answered: bfloat16 [512, 8192], P('tp', 'ctx')
The draws below stay inside these ranges and needn't reach their ends.
All inputs are finite; a program needn't handle non-finite values.
Results may differ from the reference program's by a relative error of at most 0.0049.
Values may be sent and summed in bfloat16 or wider, within the bound.
A program may use at most 64 MiB of HBM per device.

```python
import jax
import jax.numpy as jnp
from jax import lax

D = 8192
QUERY_HEADS = 64
KEY_VALUE_HEADS = 8
HEAD_SIZE = 128
BLK = 768
PROMPT_TOKENS = 512
CONTEXT_TOKENS = 24576


def loud_rows(key, base_matrix):
    pick_key, sign_key = jax.random.split(key)
    picked = jax.random.bernoulli(pick_key, 1.0 / 16.0, (base_matrix.shape[0],))
    sign_grid = jnp.where(jax.random.bernoulli(sign_key, 0.5, base_matrix.shape), 9.0, -9.0).astype(jnp.float32)
    return jnp.where(picked[:, None], sign_grid, base_matrix)


def draw_context_queries(key, part):
    key = jax.random.fold_in(key, 11)
    starting_key = jax.random.fold_in(key, 0)
    loud_key = jax.random.fold_in(key, 2)
    value_matrix = jnp.clip(2.5 * jax.random.normal(starting_key, (CONTEXT_TOKENS, QUERY_HEADS * HEAD_SIZE), jnp.float32), -9.0, 9.0)
    value_matrix = loud_rows(loud_key, value_matrix)
    return value_matrix.astype(jnp.bfloat16)


def draw_prompt_queries(key, part):
    key = jax.random.fold_in(key, 37)
    starting_key = jax.random.fold_in(key, 0)
    loud_key = jax.random.fold_in(key, 2)
    value_matrix = jnp.clip(2.5 * jax.random.normal(starting_key, (PROMPT_TOKENS, QUERY_HEADS * HEAD_SIZE), jnp.float32), -9.0, 9.0)
    value_matrix = loud_rows(loud_key, value_matrix)
    return value_matrix.astype(jnp.bfloat16)


def draw_context_keys(key, part):
    key = jax.random.fold_in(key, 23)
    starting_key = jax.random.fold_in(key, 0)
    value_matrix = jnp.clip(jax.random.normal(starting_key, (CONTEXT_TOKENS, KEY_VALUE_HEADS * HEAD_SIZE), jnp.float32), -4.0, 4.0)
    return value_matrix.astype(jnp.bfloat16)


def shard_levels(rng, extent, pieces, low, top_value):
    def one(axis_at, shards_of):
        steps = jax.random.uniform(jax.random.fold_in(jax.random.fold_in(rng, 6), axis_at), (shards_of,), jnp.float32, low / len(pieces), top_value / len(pieces))
        return jnp.repeat(jnp.exp(steps), extent[axis_at] // shards_of).reshape((-1,) + (1,) * (len(extent) - axis_at - 1))

    level = one(*pieces[0])
    for cut in pieces[1:]:
        level = level * one(*cut)
    return level


def gaussian(stream_key, extent, width, limit, shards=(), held_as=jnp.bfloat16):
    loudness = shard_levels(stream_key, extent, shards, -0.22, 0.18) if shards else 1.0
    values = jax.random.normal(stream_key, extent, jnp.float32) * width * loudness
    return jnp.minimum(jnp.maximum(values, -limit), limit).astype(held_as)


def setup_inputs(seed: int = 0) -> dict:
    keys = jax.random.split(jax.random.key(seed), 8)
    context_queries = draw_context_queries(jax.random.fold_in(keys[7], 71), 0)
    context_keys = draw_context_keys(jax.random.fold_in(keys[7], 71), 0)
    context_value_rows = gaussian(keys[2], (CONTEXT_TOKENS, KEY_VALUE_HEADS * HEAD_SIZE), 1.0, 6.0, ((0, 32), (1, 8)))
    prompt_queries = draw_prompt_queries(jax.random.fold_in(keys[7], 71), 0)
    prompt_key_rows = gaussian(keys[4], (PROMPT_TOKENS, KEY_VALUE_HEADS * HEAD_SIZE), 1.0, 4.0, ((0, 32), (1, 8)))
    prompt_value_matrix = gaussian(keys[5], (PROMPT_TOKENS, KEY_VALUE_HEADS * HEAD_SIZE), 1.0, 6.0, ((0, 32), (1, 8)))
    output_weight = gaussian(keys[6], (QUERY_HEADS * HEAD_SIZE, D), (QUERY_HEADS * HEAD_SIZE) ** -0.5, 0.0625, ((0, 8), (1, 32)))
    return dict(context_queries=context_queries, context_keys=context_keys, context_value_rows=context_value_rows, prompt_queries=prompt_queries, prompt_key_rows=prompt_key_rows, prompt_value_matrix=prompt_value_matrix, output_weight=output_weight)


def head_partial(query_rows, key_rows, value_rows, visible):
    scores = jnp.dot(query_rows, key_rows.T, preferred_element_type=jnp.float32) * (HEAD_SIZE ** -0.5)
    scores = jnp.where(visible, scores, -1e30)
    row_max = jnp.max(scores, axis=1)
    weights = jnp.exp(scores - row_max[:, None])
    row_sum = jnp.sum(weights, axis=1)
    accumulated = jnp.dot(weights.astype(jnp.bfloat16), value_rows, preferred_element_type=jnp.float32)
    return row_max, row_sum, accumulated


def columns(array, index):
    return lax.dynamic_slice_in_dim(array, index * HEAD_SIZE, HEAD_SIZE, 1)


def reference(context_queries, context_keys, context_value_rows, prompt_queries, prompt_key_rows, prompt_value_matrix, output_weight):
    query_group_width = QUERY_HEADS // KEY_VALUE_HEADS
    blocks = CONTEXT_TOKENS // BLK
    positions = jnp.arange(BLK, dtype=jnp.int32)
    causal = positions[None, :] <= positions[:, None]
    anchor_keys = context_keys[:BLK]
    anchor_values = context_value_rows[:BLK]

    def encode_block(block_index):
        row_start = block_index * BLK
        query_block = lax.dynamic_slice_in_dim(context_queries, row_start, BLK, 0)
        key_block = jnp.concatenate([anchor_keys, lax.dynamic_slice_in_dim(context_keys, row_start, BLK, 0)], axis=0)
        value_block = jnp.concatenate([anchor_values, lax.dynamic_slice_in_dim(context_value_rows, row_start, BLK, 0)], axis=0)
        visible = jnp.concatenate([jnp.broadcast_to(block_index > 0, (BLK, BLK)), causal], axis=1)

        def one_head(head_index):
            kv_head = head_index // query_group_width
            row_max, row_sum, accumulated = head_partial(columns(query_block, head_index), columns(key_block, kv_head), columns(value_block, kv_head), visible)
            return (accumulated / row_sum[:, None]).astype(jnp.bfloat16)

        per_head = lax.map(one_head, jnp.arange(QUERY_HEADS, dtype=jnp.int32))
        return jnp.transpose(per_head, (1, 0, 2)).reshape(BLK, QUERY_HEADS * HEAD_SIZE)

    encoded = lax.map(encode_block, jnp.arange(blocks, dtype=jnp.int32)).reshape(CONTEXT_TOKENS, QUERY_HEADS * HEAD_SIZE)

    share_rows = PROMPT_TOKENS // blocks
    query_positions = jnp.arange(PROMPT_TOKENS, dtype=jnp.int32)

    def block_partial(block_index):
        key_block = jnp.concatenate([lax.dynamic_slice_in_dim(context_keys, block_index * BLK, BLK, 0), lax.dynamic_slice_in_dim(prompt_key_rows, block_index * share_rows, share_rows, 0)], axis=0)
        value_block = jnp.concatenate([lax.dynamic_slice_in_dim(context_value_rows, block_index * BLK, BLK, 0), lax.dynamic_slice_in_dim(prompt_value_matrix, block_index * share_rows, share_rows, 0)], axis=0)
        own_rows = block_index * share_rows + jnp.arange(share_rows, dtype=jnp.int32)
        visible = jnp.concatenate([jnp.ones((PROMPT_TOKENS, BLK), dtype=jnp.bool_), own_rows[None, :] <= query_positions[:, None]], axis=1)

        def one_head(head_index):
            kv_head = head_index // query_group_width
            return head_partial(columns(prompt_queries, head_index), columns(key_block, kv_head), columns(value_block, kv_head), visible)

        return lax.map(one_head, jnp.arange(QUERY_HEADS, dtype=jnp.int32))

    row_max, row_sum, accumulated = lax.map(block_partial, jnp.arange(blocks, dtype=jnp.int32))
    overall = jnp.max(row_max, axis=0)
    factor = jnp.exp(row_max - overall[None])
    denominator = jnp.sum(row_sum * factor, axis=0)
    numerator = jnp.sum(accumulated * factor[..., None], axis=0)
    attended = (numerator / denominator[..., None]).astype(jnp.bfloat16)
    attended = jnp.transpose(attended, (1, 0, 2)).reshape(PROMPT_TOKENS, QUERY_HEADS * HEAD_SIZE)
    answered = jnp.dot(attended, output_weight, preferred_element_type=jnp.float32).astype(jnp.bfloat16)
    return encoded, answered
```

```python
import functools

import jax
import jax.numpy as jnp
from jax import lax
from jax.experimental import pallas as pl
from jax.experimental.pallas import tpu as pltpu
from jax.sharding import PartitionSpec as P

MESH = pl.DeviceIdType.MESH
F32 = jnp.float32
BF16 = jnp.bfloat16
HEAD = 128
HEADS = 8
NY, NZ, NT = 4, 8, 8
BLK = 768
ROWS = 16
WIDE = HEADS * HEAD
MSG = WIDE + 128
KEYS = BLK + 128
PIECE = 2 * BLK // NZ
UNIT = 384
C2 = HEAD**-0.5 * 1.4426950408889634
NEG = -1e30


def dot(a, b):
    return jnp.dot(a, b, preferred_element_type=F32)


def kernel(
    cq, ck, cv, pq, pk, pv, w,
    enc, ans,
    q_v, k_v, v_v, pk_v, pv_v, w_v,
    kt, va, kta, vaa,
    om, out_v,
    qall, att, anc,
    po, ps, r1s, r1d, r2s, r2d, r3s, r3d,
    tsend, tgot, town,
    loc, q_zs, q_fs, q_rs, q_rr,
    a_zs, a_fs, a_rs, a_rr,
    n_ss, n_ys, n_zs, n_rr,
    r1_ss, r1_rr, r2_ss, r2_rr, r3_ss, r3_rr,
    t_ss, t_rr,
):
    c = lax.axis_index("ctx")
    t = lax.axis_index("tp")
    y, z = c // NZ, c % NZ
    up, down = (y + 1) % NY, (y + NY - 1) % NY

    def remote(src, dst, ss, rr, dev):
        return pltpu.make_async_remote_copy(
            src_ref=src, dst_ref=dst, send_sem=ss, recv_sem=rr,
            device_id=dev, device_id_type=MESH,
        )

    def arrived(ref, sem):
        pltpu.make_async_copy(ref, ref, sem).wait()

    local = [
        pltpu.make_async_copy(pq, qall.at[c], loc.at[0]),
        pltpu.make_async_copy(ck, k_v, loc.at[1]),
        pltpu.make_async_copy(cv, v_v, loc.at[2]),
        pltpu.make_async_copy(cq, q_v, loc.at[3]),
        pltpu.make_async_copy(pk, pk_v, loc.at[4]),
        pltpu.make_async_copy(pv, pv_v, loc.at[5]),
        pltpu.make_async_copy(w, w_v, loc.at[6]),
    ]
    for copy in local:
        copy.start()

    barrier = pltpu.get_barrier_semaphore()
    for d in range(1, NZ):
        pl.semaphore_signal(barrier, inc=1, device_id=(y * NZ + (z + d) % NZ, t), device_id_type=MESH)
    for row in (up, down):
        pl.semaphore_signal(barrier, inc=1, device_id=(row * NZ + z, t), device_id_type=MESH)
    for d in range(1, NT):
        pl.semaphore_signal(barrier, inc=1, device_id=(c, (t + d) % NT), device_id_type=MESH)
    pl.semaphore_wait(barrier, NZ - 1 + 2 + NT - 1)

    def zed(j):
        return (z + jnp.where(j % 2 == 1, (j + 1) // 2, NZ - j // 2)) % NZ

    class Gather:
        def __init__(self, buf, zs, fs, rs, rr):
            self.buf, self.zs, self.fs, self.rs, self.rr = buf, zs, fs, rs, rr

        def zsend(self, d):
            return remote(self.buf.at[c], self.buf.at[c], self.zs.at[d], self.rr.at[c],
                          (y * NZ + (z + d) % NZ, t))

        def forward(self, j, way):
            s = y * NZ + zed(j)
            row = up if way == 0 else down
            return remote(self.buf.at[s], self.buf.at[s], self.fs.at[way, j], self.rr.at[s],
                          (row * NZ + z, t))

        def passing(self, j):
            upward = 1 - j % 2
            s = ((y + 1 + 2 * upward) % NY) * NZ + zed(j)
            row = (y + 3 - 2 * upward) % NY
            return remote(self.buf.at[s], self.buf.at[s], self.rs.at[j], self.rr.at[s],
                          (row * NZ + z, t))

        def wait(self, s):
            arrived(self.buf.at[s], self.rr.at[s])

        def start(self):
            for d in (1, 7, 2, 6, 3, 5, 4):
                self.zsend(d).start()

        def step(self, j):
            @pl.when(j > 0)
            def _():
                self.wait(y * NZ + zed(j))

            self.forward(j, 0).start()
            self.forward(j, 1).start()

        def relay(self, j):
            self.wait(down * NZ + zed(j))
            self.wait(up * NZ + zed(j))
            self.passing(j).start()

        def drain(self):
            for d in range(1, NZ):
                self.zsend(d).wait_send()

            def one(j, carry):
                self.forward(j, 0).wait_send()
                self.forward(j, 1).wait_send()
                self.passing(j).wait_send()
                return carry

            lax.fori_loop(0, NZ, one, 0)

    queries = Gather(qall, q_zs, q_fs, q_rs, q_rr)
    attended = Gather(att, a_zs, a_fs, a_rs, a_rr)

    local[0].wait()
    queries.start()

    def root_send(p):
        if p < NZ // 2:
            src = ck.at[pl.ds(p * PIECE, PIECE)]
        else:
            src = cv.at[pl.ds((p - NZ // 2) * PIECE, PIECE)]
        return remote(src, anc.at[p], n_ss.at[p], n_rr.at[p], (p, t))

    def anchor_y(row, i):
        return remote(anc.at[z], anc.at[z], n_ys.at[i], n_rr.at[z], (row * NZ + z, t))

    def anchor_z(d):
        return remote(anc.at[z], anc.at[z], n_zs.at[d], n_rr.at[z], (y * NZ + (z + d) % NZ, t))

    root_own = pltpu.make_async_copy(ck.at[pl.ds(0, PIECE)], anc.at[0], loc.at[7])

    @pl.when(c == 0)
    def _():
        root_own.start()
        for p in (1, 7, 2, 6, 3, 5, 4):
            root_send(p).start()

    def anchor_step():
        @pl.when(c == 0)
        def _():
            root_own.wait()

        @pl.when(c != 0)
        def _():
            arrived(anc.at[z], n_rr.at[z])

        @pl.when(y == 0)
        def _():
            anchor_y(1, 0).start()
            anchor_y(3, 1).start()

        @pl.when(y == 1)
        def _():
            anchor_y(2, 0).start()

        for d in (1, 7, 2, 6, 3, 5, 4):
            anchor_z(d).start()

    for copy in local[1:]:
        copy.wait()

    kt[:, :BLK] = k_v[...].T
    kt[:, BLK:] = jnp.concatenate([pk_v[...], jnp.zeros((128 - ROWS, HEAD), BF16)], axis=0).T
    va[:BLK, :HEAD] = v_v[...]
    va[BLK : BLK + ROWS, :HEAD] = pv_v[...]
    va[BLK + ROWS :, :HEAD] = jnp.zeros((128 - ROWS, HEAD), BF16)
    va[:, HEAD:] = jnp.ones((KEYS, HEAD), BF16)

    def own_head(h):
        cols = pl.ds(pl.multiple_of(h * HEAD, HEAD), HEAD)
        r = 256
        row = lax.broadcasted_iota(jnp.int32, (r, r), 0)
        col = lax.broadcasted_iota(jnp.int32, (r, r), 1)
        tiles = range(BLK // r)
        scores = []
        for i in tiles:
            s = dot(q_v[r * i : r * (i + 1), cols], kt[:, : r * (i + 1)])
            last = jnp.where(col <= row, s[:, r * i :], NEG)
            scores.append(jnp.concatenate([s[:, : r * i], last], axis=1) if i else last)
        maxima = [jnp.max(s, axis=1, keepdims=True) for s in scores]
        weights = [jnp.exp2(s * C2 - m * C2).astype(BF16) for s, m in zip(scores, maxima)]
        for i in tiles:
            om[h, r * i : r * (i + 1), : 2 * HEAD] = dot(weights[i], va[: r * (i + 1)])
            om[h, r * i : r * (i + 1), 2 * HEAD :] = jnp.broadcast_to(maxima[i], (r, HEAD))

    def loop_a(j, carry):
        queries.step(j)

        @pl.when(j > 0)
        def _():
            queries.relay(j - 1)

        @pl.when(((j == 4) & (y == 0)) | ((j == 6) & (y % 2 == 1)))
        def _():
            anchor_step()

        own_head(j)
        return carry

    lax.fori_loop(0, NZ, loop_a, 0)
    queries.relay(NZ - 1)

    @pl.when(y == 2)
    def _():
        anchor_step()

    lane = lax.broadcasted_iota(jnp.int32, (ROWS, 128), 1)
    QUAD = 4

    def prompt(row, first):
        blocks = []
        for g in range(QUAD):
            s = row * NZ + zed(first + g)
            for h in range(HEADS):
                blocks.append(qall[s, :, HEAD * h : HEAD * (h + 1)])
        s = dot(jnp.concatenate(blocks, axis=0), kt[...])
        r = lax.broadcasted_iota(jnp.int32, (HEADS * ROWS, 128), 0) % ROWS
        k = lax.broadcasted_iota(jnp.int32, (HEADS * ROWS, 128), 1)
        last = []
        for g in range(QUAD):
            ahead = (row * NZ + zed(first + g) - c) * ROWS
            tile = s[HEADS * ROWS * g : HEADS * ROWS * (g + 1), BLK:]
            last.append(jnp.where((k < ROWS) & (k <= r + ahead), tile, NEG))
        s = jnp.concatenate([s[:, :BLK], jnp.concatenate(last, axis=0)], axis=1)
        m = jnp.ceil(jnp.max(s, axis=1, keepdims=True) * (C2 / 4)) * 4
        o = dot(jnp.exp2(s * C2 - m).astype(BF16), va[...])
        for g in range(QUAD):
            stats = jnp.zeros((ROWS, 128), F32)
            for h in range(HEADS):
                at = (g * HEADS + h) * ROWS
                po[g, :, HEAD * h : HEAD * (h + 1)] = o[at : at + ROWS, :HEAD]
                stats = jnp.where(lane == h, o[at : at + ROWS, HEAD:], stats)
                stats = jnp.where(lane == 16 + h, m[at : at + ROWS], stats)
            ps[g] = stats

    def split(stats):
        high = stats.astype(BF16).astype(F32)
        rest = pltpu.roll(stats - high, 8, 1)
        return jnp.where((lane >= 8) & (lane < 16), rest, high).astype(BF16)

    def put(dst, g):
        dst[:, :WIDE] = po[g].astype(BF16)
        dst[:, WIDE:] = split(ps[g])

    def whole(stats):
        return jnp.where(lane < 8, stats + pltpu.roll(stats, 120, 1), stats)

    def merge(parts):
        top = functools.reduce(jnp.maximum, [stats for _, stats in parts])
        factors = [jnp.exp2(stats - top) for _, stats in parts]
        total = sum(stats * pltpu.roll(f, 112, 1) for (_, stats), f in zip(parts, factors))
        stats = jnp.where(lane < 8, total, jnp.where((lane >= 16) & (lane < 24), top, 0.0))
        results = []
        for h in range(HEADS):
            cols = slice(HEAD * h, HEAD * (h + 1))
            results.append(sum(
                read(cols) * f[:, 16 + h : 17 + h] for (read, _), f in zip(parts, factors)
            ))
        return results, stats

    def mine(g):
        return (lambda cols: po[g, :, cols]), ps[g]

    def got(ref):
        return (lambda cols: ref[:, cols].astype(F32)), whole(ref[:, WIDE:].astype(F32))

    def put_merged(dst, parts):
        results, stats = merge(parts)
        for h in range(HEADS):
            dst[:, HEAD * h : HEAD * (h + 1)] = results[h].astype(BF16)
        dst[:, WIDE:] = split(stats)

    def send1(j):
        row = (y + 1 + 2 * (j % 2)) % NY
        return remote(r1s.at[j], r1d.at[j], r1_ss.at[j], r1_rr.at[j], (row * NZ + z, t))

    def send2(way, j):
        row = up if way == 0 else down
        return remote(r2s.at[way, j], r2d.at[way, j], r2_ss.at[way, j], r2_rr.at[way, j], (row * NZ + z, t))

    def send3(j):
        return remote(r3s.at[j], r3d.at[j], r3_ss.at[j], r3_rr.at[j], (y * NZ + zed(j), t))

    def phase1(b, carry):
        far = (y + 2) % NY
        for g in range(QUAD):
            queries.wait(far * NZ + zed(b * QUAD + g))
        prompt(far, b * QUAD)
        for g in range(QUAD):
            put(r1s.at[b * QUAD + g], g)
            send1(b * QUAD + g).start()
        return carry

    lax.fori_loop(0, NZ // QUAD, phase1, 0)

    def phase2(b, carry):
        for way, row in ((0, up), (1, down)):
            prompt(row, b * QUAD)
            for g in range(QUAD):
                j = b * QUAD + g
                if g % 2 == way:
                    arrived(r1d.at[j], r1_rr.at[j])
                    put_merged(r2s.at[way, j], [mine(g), got(r1d.at[j])])
                else:
                    put(r2s.at[way, j], g)
                send2(way, j).start()
        return carry

    lax.fori_loop(0, NZ // QUAD, phase2, 0)

    def anchor_ready():
        for p in range(NZ):
            @pl.when(z != p)
            def _(p=p):
                arrived(anc.at[p], n_rr.at[p])
        for p in range(NZ // 2):
            kta[:, PIECE * p : PIECE * (p + 1)] = anc[p].T
            vaa[PIECE * p : PIECE * (p + 1), :HEAD] = anc[NZ // 2 + p]
        vaa[:, HEAD:] = jnp.ones((BLK, HEAD), BF16)

    seen = jnp.where(c > 0, 0.0, NEG)

    def anchor_unit(u, carry):
        h, i = u // (BLK // UNIT), u % (BLK // UNIT)
        cols = pl.ds(pl.multiple_of(h * HEAD, HEAD), HEAD)
        rows = pl.ds(pl.multiple_of(i * UNIT, UNIT), UNIT)
        s = dot(q_v[rows, cols], kta[...])
        m = jnp.max(s, axis=1, keepdims=True)
        o = dot(jnp.exp2(s * C2 - m * C2).astype(BF16), vaa[...])
        m = m + seen
        own = om[h, rows, 2 * HEAD :]
        top = jnp.maximum(m, own)
        f_own, f = jnp.exp2((own - top) * C2), jnp.exp2((m - top) * C2)
        above = om[h, rows, :HEAD] * f_own + o[:, :HEAD] * f
        below = om[h, rows, HEAD : 2 * HEAD] * f_own + o[:, HEAD:] * f
        out_v[rows, cols] = (above / below).astype(BF16)
        return carry

    UNITS = HEADS * (BLK // UNIT)

    def phase3(b):
        prompt(y, b * QUAD)
        for g in range(QUAD):
            j = b * QUAD + g
            for way in (0, 1):
                arrived(r2d.at[way, j], r2_rr.at[way, j])
            put_merged(r3s.at[j], [mine(g), got(r2d.at[0, j]), got(r2d.at[1, j])])
            if j:
                send3(j).start()

    phase3(0)
    anchor_ready()
    lax.fori_loop(0, 2, anchor_unit, 0)
    phase3(1)
    lax.fori_loop(2, UNITS - NZ, anchor_unit, 0)

    for j in range(1, NZ):
        arrived(r3d.at[j], r3_rr.at[j])
    results, stats = merge([got(r3s.at[0])] + [got(r3d.at[j]) for j in range(1, NZ)])
    for h in range(HEADS):
        att[c, :, HEAD * h : HEAD * (h + 1)] = (results[h] / stats[:, h : h + 1]).astype(BF16)

    attended.start()

    def loop_b(j, carry):
        attended.step(j)

        @pl.when(j > 0)
        def _():
            attended.relay(j - 1)

        anchor_unit(UNITS - NZ + j, carry)
        return carry

    lax.fori_loop(0, NZ, loop_b, 0)
    attended.relay(NZ - 1)
    enc_out = pltpu.make_async_copy(out_v, enc, loc.at[8])
    enc_out.start()

    half = 2 * NZ * ROWS // 4

    def tp_send(to):
        return remote(tsend.at[to], tgot.at[t], t_ss.at[to], t_rr.at[t], (c, to))

    for g in (0, 1, 3, 2):
        row = (y + g) % NY
        if g == 2:
            for j in range(NZ):
                attended.wait(row * NZ + zed(j))
        a = jnp.concatenate([att[row * NZ + i] for i in range(NZ)], axis=0)
        part = dot(a, w_v[...])
        for b in range(2):
            to = 2 * row + b
            piece = part[half * b : half * (b + 1)]

            @pl.when(to == t)
            def _(piece=piece):
                town[...] = piece

            @pl.when(to != t)
            def _(piece=piece, to=to):
                tsend[to] = piece.astype(BF16)
                tp_send(to).start()

    for d in range(1, NT):
        other = (t + d) % NT
        arrived(tgot.at[other], t_rr.at[other])
    ans[...] = (town[...] + sum(tgot[(t + d) % NT].astype(F32) for d in range(1, NT))).astype(BF16)

    queries.drain()
    attended.drain()
    for d in range(1, NZ):
        anchor_z(d).wait_send()

    @pl.when(c == 0)
    def _():
        for p in range(1, NZ):
            root_send(p).wait_send()

    @pl.when(y == 0)
    def _():
        anchor_y(1, 0).wait_send()
        anchor_y(3, 1).wait_send()

    @pl.when(y == 1)
    def _():
        anchor_y(2, 0).wait_send()

    for j in range(NZ):
        send1(j).wait_send()
        send2(0, j).wait_send()
        send2(1, j).wait_send()
        if j:
            send3(j).wait_send()
    for d in range(1, NT):
        tp_send((t + d) % NT).wait_send()
    enc_out.wait()


def on_device(cq, ck, cv, pq, pk, pv, w):
    vm, dma = pltpu.VMEM, pltpu.SemaphoreType.DMA
    feats = w.shape[1]
    half = 2 * NZ * ROWS // 4
    any_space = pl.BlockSpec(memory_space=pl.ANY)
    return pl.pallas_call(
        kernel,
        out_shape=(
            jax.ShapeDtypeStruct((BLK, WIDE), BF16),
            jax.ShapeDtypeStruct((half, feats), BF16),
        ),
        in_specs=[any_space] * 7,
        out_specs=(any_space, pl.BlockSpec(memory_space=pltpu.VMEM)),
        scratch_shapes=[
            vm((BLK, WIDE), BF16), vm((BLK, HEAD), BF16), vm((BLK, HEAD), BF16),
            vm((ROWS, HEAD), BF16), vm((ROWS, HEAD), BF16), vm((WIDE, feats), BF16),
            vm((HEAD, KEYS), BF16), vm((KEYS, 2 * HEAD), BF16),
            vm((HEAD, BLK), BF16), vm((BLK, 2 * HEAD), BF16),
            vm((HEADS, BLK, 3 * HEAD), F32), vm((BLK, WIDE), BF16),
            vm((NY * NZ, ROWS, WIDE), BF16), vm((NY * NZ, ROWS, WIDE), BF16),
            vm((NZ, PIECE, HEAD), BF16),
            vm((4, ROWS, WIDE), F32), vm((4, ROWS, 128), F32),
            vm((NZ, ROWS, MSG), BF16), vm((NZ, ROWS, MSG), BF16),
            vm((2, NZ, ROWS, MSG), BF16), vm((2, NZ, ROWS, MSG), BF16),
            vm((NZ, ROWS, MSG), BF16), vm((NZ, ROWS, MSG), BF16),
            vm((NT, half, feats), BF16), vm((NT, half, feats), BF16), vm((half, feats), F32),
            dma((9,)), dma((NZ,)), dma((2, NZ)), dma((NZ,)), dma((NY * NZ,)),
            dma((NZ,)), dma((2, NZ)), dma((NZ,)), dma((NY * NZ,)),
            dma((NZ,)), dma((2,)), dma((NZ,)), dma((NZ,)),
            dma((NZ,)), dma((NZ,)), dma((2, NZ)), dma((2, NZ)), dma((NZ,)), dma((NZ,)),
            dma((NT,)), dma((NT,)),
        ],
        compiler_params=pltpu.CompilerParams(
            collective_id=0, has_side_effects=True, vmem_limit_bytes=56 * 2**20
        ),
        cost_estimate=pl.CostEstimate(flops=12 * 10**9, bytes_accessed=5 * 10**6, transcendentals=11 * 10**6),
        name="star",
    )(cq, ck, cv, pq, pk, pv, w)


def solution(mesh):
    placed = (P("ctx", "tp"),) * 6 + (P("tp", "ctx"),)
    return jax.shard_map(
        on_device,
        mesh=mesh,
        in_specs=placed,
        out_specs=(P("ctx", "tp"), P("tp", "ctx")),
        check_vma=False,
    )
```

```python
import functools

import jax
import jax.numpy as jnp
from jax import lax
from jax.experimental import pallas as pl
from jax.experimental.pallas import tpu as pltpu
from jax.sharding import PartitionSpec as P

MESH = pl.DeviceIdType.MESH
F32 = jnp.float32
BF16 = jnp.bfloat16
HEAD = 128
HEADS = 8
NY, NZ, NX, NK = 4, 8, 4, 2
BLK = 768
ROWS = 16
WIDE = HEADS * HEAD
MSG = WIDE + 128
HELD = BLK + ROWS
KEYS = BLK + 128
PIECE = 2 * BLK // NZ
UNIT = 384
UNITS = HEADS * (BLK // UNIT)
HALF = NZ * ROWS // 2
FEATS = 256
C2 = HEAD**-0.5 * 1.4426950408889634
NEG = -1e30
FAR_FIRST = (4, 3, 5, 2, 6, 1, 7)


def dot(a, b):
    return jnp.dot(a, b, preferred_element_type=F32)


def kernel(
    cq, ck, cv, pq, pk, pv, w,
    enc, ans,
    q_v, kall, vall, wall, kt, kta, vaa, om, out_v,
    qz, qst, po, pm, att, anc, r3s, r3d,
    pacc, pgot, fsend, fgot,
    loc, q_ss, q_rr, k_ss, k_rr, v_ss, v_rr, w_ss, w_rr,
    n_ss, n_ys, n_zs, n_rr, r3_ss, r3_rr, a_ss, a_rr, c_ss, c_rr, f_ss, f_rr,
):
    c = lax.axis_index("ctx")
    t = lax.axis_index("tp")
    y, z = c // NZ, c % NZ
    x, core = t // NK, t % NK
    up, down, far = (y + 1) % NY, (y + NY - 1) % NY, (y + 2) % NY

    def remote(src, dst, ss, rr, dev):
        return pltpu.make_async_remote_copy(
            src_ref=src, dst_ref=dst, send_sem=ss, recv_sem=rr,
            device_id=dev, device_id_type=MESH,
        )

    def arrived(ref, sem):
        pltpu.make_async_copy(ref, ref, sem).wait()

    def at_z(d):
        return (y * NZ + (z + d) % NZ, t)

    def at_y(row):
        return (row * NZ + z, t)

    local_q = pltpu.make_async_copy(pq, qz.at[z], loc.at[0])
    local_kv = [
        pltpu.make_async_copy(ck, kall.at[y, pl.ds(0, BLK)], loc.at[1]),
        pltpu.make_async_copy(pk, kall.at[y, pl.ds(BLK, ROWS)], loc.at[2]),
        pltpu.make_async_copy(cv, vall.at[y, pl.ds(0, BLK), pl.ds(0, HEAD)], loc.at[3]),
        pltpu.make_async_copy(pv, vall.at[y, pl.ds(BLK, ROWS), pl.ds(0, HEAD)], loc.at[4]),
    ]
    local_rest = [
        pltpu.make_async_copy(cq, q_v, loc.at[5]),
        pltpu.make_async_copy(w, wall.at[y], loc.at[6]),
    ]
    local_q.start()
    for copy in local_kv + local_rest:
        copy.start()

    barrier = pltpu.get_barrier_semaphore()

    def greet(dev):
        pl.semaphore_signal(barrier, inc=1, device_id=dev, device_id_type=MESH)

    for d in range(1, NZ):
        greet(at_z(d))
    greet(at_y(up))
    greet(at_y(down))
    greet((c, x * NK + 1 - core))
    for other in range(NX):
        @pl.when((other != x) | (x != y))
        def _(other=other):
            greet((x * NZ + z, other * NK + core))
    pl.semaphore_wait(barrier, NZ - 1 + 2 + 1 + NY - jnp.where(x == y, 1, 0))

    def q_send(d):
        return remote(qz.at[z], qz.at[z], q_ss.at[d], q_rr.at[z], at_z(d))

    local_q.wait()
    for d in FAR_FIRST:
        q_send(d).start()

    def root_send(p):
        if p < NZ // 2:
            src = ck.at[pl.ds(p * PIECE, PIECE)]
        else:
            src = cv.at[pl.ds((p - NZ // 2) * PIECE, PIECE)]
        return remote(src, anc.at[p], n_ss.at[p], n_rr.at[p], (p, t))

    def anchor_y(row, i):
        return remote(anc.at[z], anc.at[z], n_ys.at[i], n_rr.at[z], at_y(row))

    def anchor_z(d):
        return remote(anc.at[z], anc.at[z], n_zs.at[d], n_rr.at[z], at_z(d))

    root_own = pltpu.make_async_copy(ck.at[pl.ds(0, PIECE)], anc.at[0], loc.at[7])

    @pl.when(c == 0)
    def _():
        root_own.start()
        for p in FAR_FIRST:
            root_send(p).start()

    def anchor_step():
        @pl.when(c == 0)
        def _():
            root_own.wait()

        @pl.when(c != 0)
        def _():
            arrived(anc.at[z], n_rr.at[z])

        @pl.when(y == 0)
        def _():
            anchor_y(1, 0).start()
            anchor_y(3, 1).start()

        @pl.when(y == 1)
        def _():
            anchor_y(2, 0).start()

        for d in FAR_FIRST:
            anchor_z(d).start()

    def keys_of(row):
        return kall.at[row, pl.ds(0, HELD)]

    def values_of(row):
        return vall.at[row, pl.ds(0, HELD), pl.ds(0, HEAD)]

    def k_send(row, to, i):
        return remote(keys_of(row), keys_of(row), k_ss.at[i], k_rr.at[row], at_y(to))

    def v_send(row, to, i):
        return remote(values_of(row), values_of(row), v_ss.at[i], v_rr.at[row], at_y(to))

    for copy in local_kv:
        copy.wait()
    k_send(y, up, 0).start()
    v_send(y, down, 1).start()
    v_send(y, up, 0).start()
    k_send(y, down, 1).start()

    W_ROWS = WIDE // 2

    def w_send(part, row, to, i):
        ref = wall.at[row, pl.ds(part * W_ROWS, W_ROWS)]
        return remote(ref, ref, w_ss.at[part, i], w_rr.at[part, row], at_y(to))

    def w_wait(part, row):
        arrived(wall.at[row, pl.ds(part * W_ROWS, W_ROWS)], w_rr.at[part, row])

    for b in range(NY):
        kall[b, HELD:] = jnp.zeros((KEYS - HELD, HEAD), BF16)
        vall[b, HELD:, :HEAD] = jnp.zeros((KEYS - HELD, HEAD), BF16)
        vall[b, :, HEAD:] = jnp.ones((KEYS, HEAD), BF16)
    vaa[:, HEAD:] = jnp.ones((BLK, HEAD), BF16)
    po[...] = jnp.zeros(po.shape, F32)
    pm[...] = jnp.full(pm.shape, NEG, F32)
    kt[y] = kall[y].T
    for copy in local_rest:
        copy.wait()

    def own_head(h):
        cols = pl.ds(pl.multiple_of(h * HEAD, HEAD), HEAD)
        r = 256
        row = lax.broadcasted_iota(jnp.int32, (r, r), 0)
        col = lax.broadcasted_iota(jnp.int32, (r, r), 1)
        tiles = range(BLK // r)
        scores = []
        for i in tiles:
            s = dot(q_v[r * i : r * (i + 1), cols], kt[y, :, : r * (i + 1)])
            last = jnp.where(col <= row, s[:, r * i :], NEG)
            scores.append(jnp.concatenate([s[:, : r * i], last], axis=1) if i else last)
        maxima = [jnp.max(s, axis=1, keepdims=True) for s in scores]
        weights = [jnp.exp2(s * C2 - m * C2).astype(BF16) for s, m in zip(scores, maxima)]
        for i in tiles:
            om[h, r * i : r * (i + 1), : 2 * HEAD] = dot(weights[i], vall[y, : r * (i + 1)])
            om[h, r * i : r * (i + 1), 2 * HEAD :] = jnp.broadcast_to(maxima[i], (r, HEAD))

    def loop_a(j, carry):
        own_head(j)

        @pl.when(j == 3)
        def _():
            arrived(keys_of(down), k_rr.at[down])
            k_send(down, up, 2).start()
            arrived(values_of(up), v_rr.at[up])
            v_send(up, down, 2).start()

        @pl.when(((j == 4) & (y == 0)) | ((j == 6) & (y % 2 == 1)))
        def _():
            anchor_step()

        return carry

    lax.fori_loop(0, HEADS, loop_a, 0)

    for part in range(2):
        w_send(part, y, up, 0).start()
        w_send(part, y, down, 1).start()

    def turn(j):
        return (z + 2 + j) % NZ

    for d in range(1, NZ):
        arrived(qz.at[(z + d) % NZ], q_rr.at[(z + d) % NZ])
    for j in range(NZ):
        for h in range(HEADS):
            qst[(j * HEADS + h) * ROWS : (j * HEADS + h + 1) * ROWS] = qz[turn(j), :, HEAD * h : HEAD * (h + 1)]
    arrived(values_of(down), v_rr.at[down])
    arrived(keys_of(up), k_rr.at[up])
    kt[down] = kall[down].T
    kt[up] = kall[up].T

    QUAD = 4
    STACK = HEADS * ROWS

    def prompt(s_at, carry):
        a, i = s_at // NY, s_at % NY
        b = (y + jnp.where(i == 0, 0, jnp.where(i == 1, 3, i - 1))) % NY

        @pl.when((s_at == 2) & (y == 2))
        def _():
            anchor_step()

        @pl.when(s_at == 3)
        def _():
            arrived(keys_of(far), k_rr.at[far])
            arrived(values_of(far), v_rr.at[far])
            kt[far] = kall[far].T

        rows = pl.ds(pl.multiple_of(a * (QUAD * STACK), QUAD * STACK), QUAD * STACK)
        s = dot(qst[rows], kt[b])
        r = lax.broadcasted_iota(jnp.int32, (STACK, 128), 0) % ROWS
        k = lax.broadcasted_iota(jnp.int32, (STACK, 128), 1)
        last = []
        for g in range(QUAD):
            ahead = (y * NZ + turn(a * QUAD + g) - (b * NZ + z)) * ROWS
            last.append(jnp.where((k < ROWS) & (k <= r + ahead), s[STACK * g : STACK * (g + 1), BLK:], NEG))
        s = jnp.concatenate([s[:, :BLK], jnp.concatenate(last, axis=0)], axis=1)
        m = jnp.max(s, axis=1, keepdims=True) * C2
        o = dot(jnp.exp2(s * C2 - m).astype(BF16), vall[b])
        old = pm[rows]
        top = jnp.maximum(old, m)
        f_old, f = jnp.exp2(old - top), jnp.exp2(m - top)
        pm[rows] = top
        po[rows, :HEAD] = po[rows, :HEAD] * f_old + o[:, :HEAD] * f
        po[rows, HEAD:] = po[rows, HEAD:] * f_old + o[:, HEAD:] * f

        @pl.when(i == NY - 1)
        def _():
            for g in range(QUAD):
                send_partial(a * QUAD + g)

        return carry

    lane = lax.broadcasted_iota(jnp.int32, (ROWS, 128), 1)

    def r3_send(j):
        return remote(r3s.at[j], r3d.at[j], r3_ss.at[j], r3_rr.at[j], at_z(2 + j))

    def send_partial(j):
        stats = jnp.zeros((ROWS, 128), F32)
        for h in range(HEADS):
            rows = pl.ds(pl.multiple_of((j * HEADS + h) * ROWS, ROWS), ROWS)
            m = pm[rows]
            even = jnp.ceil(m * 0.25) * 4
            f = jnp.exp2(m - even)
            r3s[j, :, HEAD * h : HEAD * (h + 1)] = (po[rows, :HEAD] * f).astype(BF16)
            total = po[rows, HEAD:] * f
            high = total.astype(BF16).astype(F32)
            stats = jnp.where(lane == h, high, stats)
            stats = jnp.where(lane == 8 + h, total - high, stats)
            stats = jnp.where(lane == 16 + h, even, stats)
        r3s[j, :, WIDE:] = stats.astype(BF16)

        @pl.when(j != 6)
        def _():
            r3_send(j).start()

    lax.fori_loop(0, 2 * NY, prompt, 0)

    w_wait(0, down)
    w_send(0, down, up, 2).start()
    w_wait(1, up)
    w_send(1, up, down, 2).start()

    for d in range(1, NZ):
        arrived(anc.at[(z + d) % NZ], n_rr.at[(z + d) % NZ])
    for p in range(NZ // 2):
        kta[:, PIECE * p : PIECE * (p + 1)] = anc[p].T
        vaa[PIECE * p : PIECE * (p + 1), :HEAD] = anc[NZ // 2 + p]

    seen = jnp.where(c > 0, 0.0, NEG)

    def anchor_unit(u, carry):
        h, i = u // (BLK // UNIT), u % (BLK // UNIT)
        cols = pl.ds(pl.multiple_of(h * HEAD, HEAD), HEAD)
        rows = pl.ds(pl.multiple_of(i * UNIT, UNIT), UNIT)
        s = dot(q_v[rows, cols], kta[...])
        m = jnp.max(s, axis=1, keepdims=True)
        o = dot(jnp.exp2(s * C2 - m * C2).astype(BF16), vaa[...])
        m = m + seen
        own = om[h, rows, 2 * HEAD :]
        top = jnp.maximum(m, own)
        f_own, f = jnp.exp2((own - top) * C2), jnp.exp2((m - top) * C2)
        above = om[h, rows, :HEAD] * f_own + o[:, :HEAD] * f
        below = om[h, rows, HEAD : 2 * HEAD] * f_own + o[:, HEAD:] * f
        out_v[rows, cols] = (above / below).astype(BF16)
        return carry

    lax.fori_loop(0, RS_UNITS, anchor_unit, 0)

    for j in range(NZ):
        if j != 6:
            arrived(r3d.at[j], r3_rr.at[j])
    parts = [r3s if j == 6 else r3d for j in range(NZ)]
    stats = [parts[j][j, :, WIDE:].astype(F32) for j in range(NZ)]
    top = functools.reduce(jnp.maximum, stats)
    factors = [jnp.exp2(s - top) for s in stats]
    total = sum(
        (s + pltpu.roll(s, 120, 1)) * pltpu.roll(f, 112, 1) for s, f in zip(stats, factors)
    )
    for h in range(HEADS):
        cols = slice(HEAD * h, HEAD * (h + 1))
        merged = sum(
            parts[j][j, :, cols].astype(F32) * factors[j][:, 16 + h : 17 + h] for j in range(NZ)
        )
        att[z, :, cols] = (merged / total[:, h : h + 1]).astype(BF16)

    def a_send(d):
        return remote(att.at[z], att.at[z], a_ss.at[d], a_rr.at[z], at_z(d))

    for d in FAR_FIRST:
        a_send(d).start()

    lax.fori_loop(RS_UNITS, RS_UNITS + AG_UNITS, anchor_unit, 0)

    for part in range(2):
        if part == 0:
            w_wait(0, up)
            w_wait(1, down)
        w_wait(part, far)
    for d in range(1, NZ):
        arrived(att.at[(z + d) % NZ], a_rr.at[(z + d) % NZ])
    rows = jnp.concatenate([att[i] for i in range(NZ)], axis=0)
    for b in range(NY):
        part = dot(rows, wall[b])
        for i in range(2):
            pacc[i, :, FEATS * b : FEATS * (b + 1)] = part[HALF * i : HALF * (i + 1)]

    c_send = remote(pacc.at[1 - core], pgot, c_ss, c_rr, (c, x * NK + 1 - core))
    c_send.start()
    c_send.wait_recv()

    def f_send(row):
        return remote(fsend.at[row], fgot.at[x], f_ss.at[row], f_rr.at[x], (row * NZ + z, y * NK + core))

    for row in range(NY):
        cols = slice(FEATS * row, FEATS * (row + 1))
        piece = pacc[core, :, cols] + pgot[:, cols]
        home = (x == y) & (y == row)

        @pl.when(home)
        def _(piece=piece):
            fgot[x] = piece.astype(BF16)

        @pl.when(jnp.logical_not(home))
        def _(piece=piece, row=row):
            fsend[row] = piece.astype(BF16)
            f_send(row).start()

    lax.fori_loop(RS_UNITS + AG_UNITS, UNITS, anchor_unit, 0)
    enc_out = pltpu.make_async_copy(out_v, enc, loc.at[8])
    enc_out.start()

    for other in range(NX):
        @pl.when((other != x) | (x != y))
        def _(other=other):
            arrived(fgot.at[other], f_rr.at[other])
    ans[...] = sum(fgot[i].astype(F32) for i in range(NX)).astype(BF16)

    for d in range(1, NZ):
        q_send(d).wait_send()
        anchor_z(d).wait_send()
        a_send(d).wait_send()

    @pl.when(c == 0)
    def _():
        for p in range(1, NZ):
            root_send(p).wait_send()

    @pl.when(y == 0)
    def _():
        anchor_y(1, 0).wait_send()
        anchor_y(3, 1).wait_send()

    @pl.when(y == 1)
    def _():
        anchor_y(2, 0).wait_send()

    for i, row in enumerate((y, y, down)):
        k_send(row, up, i).wait_send()
        w_send(0, row, up, i).wait_send()
        w_send(1, row, up, i).wait_send()
        v_send(row, up, i).wait_send()
    for j in range(NZ):
        if j != 6:
            r3_send(j).wait_send()
    c_send.wait_send()
    for row in range(NY):
        @pl.when((x != y) | (y != row))
        def _(row=row):
            f_send(row).wait_send()
    enc_out.wait()


RS_UNITS = 6
AG_UNITS = 6


def on_device(cq, ck, cv, pq, pk, pv, w):
    vm, dma = pltpu.VMEM, pltpu.SemaphoreType.DMA
    any_space = pl.BlockSpec(memory_space=pl.ANY)
    return pl.pallas_call(
        kernel,
        out_shape=(
            jax.ShapeDtypeStruct((BLK, WIDE), BF16),
            jax.ShapeDtypeStruct((HALF, FEATS), BF16),
        ),
        in_specs=[any_space] * 7,
        out_specs=(any_space, pl.BlockSpec(memory_space=pltpu.VMEM)),
        scratch_shapes=[
            vm((BLK, WIDE), BF16), vm((NY, KEYS, HEAD), BF16), vm((NY, KEYS, 2 * HEAD), BF16),
            vm((NY, WIDE, FEATS), BF16), vm((NY, HEAD, KEYS), BF16),
            vm((HEAD, BLK), BF16), vm((BLK, 2 * HEAD), BF16),
            vm((HEADS, BLK, 3 * HEAD), F32), vm((BLK, WIDE), BF16),
            vm((NZ, ROWS, WIDE), BF16), vm((NZ * HEADS * ROWS, HEAD), BF16),
            vm((NZ * HEADS * ROWS, 2 * HEAD), F32), vm((NZ * HEADS * ROWS, HEAD), F32),
            vm((NZ, ROWS, WIDE), BF16), vm((NZ, PIECE, HEAD), BF16),
            vm((NZ, ROWS, MSG), BF16), vm((NZ, ROWS, MSG), BF16),
            vm((2, HALF, NY * FEATS), F32), vm((HALF, NY * FEATS), F32),
            vm((NY, HALF, FEATS), BF16), vm((NX, HALF, FEATS), BF16),
            dma((9,)), dma((NZ,)), dma((NZ,)), dma((3,)), dma((NY,)), dma((3,)), dma((NY,)),
            dma((2, 3)), dma((2, NY)),
            dma((NZ,)), dma((2,)), dma((NZ,)), dma((NZ,)), dma((NZ,)), dma((NZ,)),
            dma((NZ,)), dma((NZ,)), dma, dma, dma((NY,)), dma((NX,)),
        ],
        compiler_params=pltpu.CompilerParams(
            collective_id=0, has_side_effects=True, vmem_limit_bytes=56 * 2**20
        ),
        cost_estimate=pl.CostEstimate(flops=12 * 10**9, bytes_accessed=5 * 10**6, transcendentals=11 * 10**6),
        name="star",
    )(cq, ck, cv, pq, pk, pv, w)


def solution(mesh):
    placed = (P("ctx", "tp"),) * 6 + (P("tp", "ctx"),)
    return jax.shard_map(
        on_device,
        mesh=mesh,
        in_specs=placed,
        out_specs=(P("ctx", "tp"), P("tp", "ctx")),
        check_vma=False,
    )
```

```python
import functools

import jax
import jax.numpy as jnp
from jax import lax
from jax.experimental import pallas as pl
from jax.experimental.pallas import tpu as pltpu
from jax.sharding import PartitionSpec as P

MESH = pl.DeviceIdType.MESH
F32 = jnp.float32
BF16 = jnp.bfloat16
HEAD = 128
HEADS = 8
NY, NZ, NX, NK = 4, 8, 4, 2
BLK = 768
ROWS = 16
WIDE = HEADS * HEAD
MSG = WIDE + 128
HELD = BLK + ROWS
KEYS = BLK + 128
PIECE = 2 * BLK // NZ
QUARTER = PIECE // NY
EARLY = 3
AG_UNITS = 3
HALF = NZ * ROWS // 2
FEATS = 256
C2 = HEAD**-0.5 * 1.4426950408889634
NEG = -1e30
FAR_FIRST = (4, 3, 5, 2, 6, 1, 7)


def dot(a, b):
    return jnp.dot(a, b, preferred_element_type=F32)


def kernel(
    cq, ck, cv, pq, pk, pv, w,
    enc, ans,
    q_v, kall, vgot, vall, wall, kt, kta, vaa, om, out_v,
    qz, qst, po, pm, att, stage, anc, r3s, r3d,
    pacc, pgot, fsend, fgot,
    loc, q_ss, q_rr, k_ss, k_rr, v_ss, v_rr, w_ss, w_rr,
    n_ss, n_qs, n_zs, n_ys, n_rr, n_zr, n_yr, r3_ss, r3_rr, a_ss, a_rr, c_ss, c_rr, f_ss, f_rr,
):
    c = lax.axis_index("ctx")
    t = lax.axis_index("tp")
    y, z = c // NZ, c % NZ
    x, core = t // NK, t % NK
    up, down, far = (y + 1) % NY, (y + NY - 1) % NY, (y + 2) % NY

    def remote(src, dst, ss, rr, dev):
        return pltpu.make_async_remote_copy(
            src_ref=src, dst_ref=dst, send_sem=ss, recv_sem=rr,
            device_id=dev, device_id_type=MESH,
        )

    def arrived(ref, sem):
        pltpu.make_async_copy(ref, ref, sem).wait()

    def at_z(d):
        return (y * NZ + (z + d) % NZ, t)

    def at_y(row):
        return (row * NZ + z, t)

    local_q = pltpu.make_async_copy(pq, qz.at[z], loc.at[0])
    local_kv = [
        pltpu.make_async_copy(ck, kall.at[y, pl.ds(0, BLK)], loc.at[1]),
        pltpu.make_async_copy(pk, kall.at[y, pl.ds(BLK, ROWS)], loc.at[2]),
        pltpu.make_async_copy(cv, vgot.at[y, pl.ds(0, BLK)], loc.at[3]),
        pltpu.make_async_copy(pv, vgot.at[y, pl.ds(BLK, ROWS)], loc.at[4]),
    ]
    local_rest = [
        pltpu.make_async_copy(cq, q_v, loc.at[5]),
        pltpu.make_async_copy(w, wall.at[y], loc.at[6]),
    ]
    local_q.start()
    for copy in local_kv + local_rest:
        copy.start()

    barrier = pltpu.get_barrier_semaphore()

    def greet(dev):
        pl.semaphore_signal(barrier, inc=1, device_id=dev, device_id_type=MESH)

    for d in range(1, NZ):
        greet(at_z(d))
    greet(at_y(up))
    greet(at_y(down))
    greet(at_y(far))
    greet((c, x * NK + 1 - core))
    for other in range(NX):
        @pl.when((other != x) | (x != y))
        def _(other=other):
            greet((x * NZ + z, other * NK + core))
    pl.semaphore_wait(barrier, NZ - 1 + 3 + 1 + NY - jnp.where(x == y, 1, 0))

    def q_send(d):
        return remote(qz.at[z], qz.at[z], q_ss.at[d], q_rr.at[z], at_z(d))


    def root_send(p):
        if p < NZ // 2:
            src = ck.at[pl.ds(p * PIECE, PIECE)]
        else:
            src = cv.at[pl.ds((p - NZ // 2) * PIECE, PIECE)]
        return remote(src, stage, n_ss.at[p], n_rr.at[0], (p, t))

    def quarter_send(row):
        return remote(stage.at[pl.ds(row * QUARTER, QUARTER)], anc.at[row, z], n_qs.at[row], n_rr.at[1], at_y(row))

    def anchor_z(d):
        return remote(anc.at[y, z], anc.at[y, z], n_zs.at[d], n_zr.at[z], at_z(d))

    def anchor_y(row, i):
        return remote(anc.at[y], anc.at[y], n_ys.at[i], n_yr.at[y], at_y(row))

    root_own = pltpu.make_async_copy(ck.at[pl.ds(0, PIECE)], stage, loc.at[7])

    @pl.when(c == 0)
    def _():
        root_own.start()
        for p in FAR_FIRST:
            root_send(p).start()

    local_q.wait()
    for d in FAR_FIRST:
        q_send(d).start()

    def anchor_quarters():
        @pl.when(c == 0)
        def _():
            root_own.wait()

        @pl.when(c != 0)
        def _():
            arrived(stage, n_rr.at[0])

        for row in (2, 1, 3):
            quarter_send(row).start()
        anc[0, z] = stage[:QUARTER]
        for d in FAR_FIRST:
            anchor_z(d).start()

    def anchor_along_z():
        arrived(anc.at[y, z], n_rr.at[1])
        for d in FAR_FIRST:
            anchor_z(d).start()

    def anchor_along_y():
        for d in range(1, NZ):
            arrived(anc.at[y, (z + d) % NZ], n_zr.at[(z + d) % NZ])
        for i, row in enumerate((far, up, down)):
            anchor_y(row, i).start()

    def keys_of(row):
        return kall.at[row, pl.ds(0, HELD)]

    def values_of(row):
        return vgot.at[row]

    def spread_values(row):
        vall[row, :HELD, :HEAD] = vgot[row]

    def k_send(row, to, i):
        return remote(keys_of(row), keys_of(row), k_ss.at[i], k_rr.at[row], at_y(to))

    def v_send(row, to, i):
        return remote(values_of(row), values_of(row), v_ss.at[i], v_rr.at[row], at_y(to))

    for copy in local_kv:
        copy.wait()
    k_send(y, up, 0).start()
    v_send(y, down, 1).start()
    v_send(y, up, 0).start()
    k_send(y, down, 1).start()

    W_ROWS = WIDE // 2

    def w_send(part, row, to, i):
        ref = wall.at[row, pl.ds(part * W_ROWS, W_ROWS)]
        return remote(ref, ref, w_ss.at[part, i], w_rr.at[part, row], at_y(to))

    def w_wait(part, row):
        arrived(wall.at[row, pl.ds(part * W_ROWS, W_ROWS)], w_rr.at[part, row])

    for b in range(NY):
        kall[b, HELD:] = jnp.zeros((KEYS - HELD, HEAD), BF16)
        vall[b, HELD:, :HEAD] = jnp.zeros((KEYS - HELD, HEAD), BF16)
        vall[b, :, HEAD:] = jnp.ones((KEYS, HEAD), BF16)
    vaa[:, HEAD:] = jnp.ones((BLK, HEAD), BF16)
    po[...] = jnp.zeros(po.shape, F32)
    pm[...] = jnp.full(pm.shape, NEG, F32)
    kt[y] = kall[y].T
    spread_values(y)
    for copy in local_rest:
        copy.wait()

    def own_head(h):
        cols = pl.ds(pl.multiple_of(h * HEAD, HEAD), HEAD)
        r = 256
        row = lax.broadcasted_iota(jnp.int32, (r, r), 0)
        col = lax.broadcasted_iota(jnp.int32, (r, r), 1)
        tiles = range(BLK // r)
        scores = []
        for i in tiles:
            s = dot(q_v[r * i : r * (i + 1), cols], kt[y, :, : r * (i + 1)])
            last = jnp.where(col <= row, s[:, r * i :], NEG)
            scores.append(jnp.concatenate([s[:, : r * i], last], axis=1) if i else last)
        maxima = [jnp.max(s, axis=1, keepdims=True) for s in scores]
        weights = [jnp.exp2(s * C2 - m * C2).astype(BF16) for s, m in zip(scores, maxima)]
        for i in tiles:
            om[h, r * i : r * (i + 1), : 2 * HEAD] = dot(weights[i], vall[y, : r * (i + 1)])
            om[h, r * i : r * (i + 1), 2 * HEAD :] = jnp.broadcast_to(maxima[i], (r, HEAD))

    def loop_a(j, carry):
        own_head(2 * j)
        own_head(2 * j + 1)

        return carry

    lax.fori_loop(0, EARLY, loop_a, 0)
    arrived(keys_of(down), k_rr.at[down])
    k_send(down, up, 2).start()
    arrived(values_of(up), v_rr.at[up])
    v_send(up, down, 2).start()

    @pl.when(y == 0)
    def _():
        anchor_quarters()

    w_send(0, y, up, 0).start()
    w_send(1, y, down, 1).start()
    w_send(1, y, up, 0).start()
    w_send(0, y, down, 1).start()

    def turn(j):
        return (z + 2 + j) % NZ

    for d in range(1, NZ):
        arrived(qz.at[(z + d) % NZ], q_rr.at[(z + d) % NZ])
    for j in range(NZ):
        for h in range(HEADS):
            qst[(j * HEADS + h) * ROWS : (j * HEADS + h + 1) * ROWS] = qz[turn(j), :, HEAD * h : HEAD * (h + 1)]
    kt[down] = kall[down].T

    QUAD = 4
    STACK = HEADS * ROWS

    def prompt(i, carry):
        halves = (i // 3, jnp.where((i == 0) | (i > 1), 1, 0))
        steps = (jnp.where(i == 0, 0, jnp.where(i == 1, 3, jnp.where(i == 2, 2, 1))),
                 jnp.where(i == 0, 0, jnp.where(i == 1, 1, jnp.where(i == 2, 3, 2))))

        @pl.when(i == 1)
        def _():
            arrived(values_of(down), v_rr.at[down])
            arrived(keys_of(up), k_rr.at[up])
            kt[up] = kall[up].T
            spread_values(down)
            spread_values(up)

        @pl.when(i == 2)
        def _():
            arrived(keys_of(far), k_rr.at[far])
            arrived(values_of(far), v_rr.at[far])
            kt[far] = kall[far].T
            spread_values(far)

        @pl.when((i == 2) & (y != 0))
        def _():
            anchor_along_z()

        r = lax.broadcasted_iota(jnp.int32, (STACK, 128), 0) % ROWS
        k = lax.broadcasted_iota(jnp.int32, (STACK, 128), 1)
        pairs = [
            (a, (y + step) % NY, pl.ds(pl.multiple_of(a * (QUAD * STACK), QUAD * STACK), QUAD * STACK))
            for a, step in zip(halves, steps)
        ]
        scores = []
        for a, b, rows in pairs:
            s = dot(qst[rows], kt[b])
            last = []
            for g in range(QUAD):
                ahead = (y * NZ + turn(a * QUAD + g) - (b * NZ + z)) * ROWS
                last.append(jnp.where((k < ROWS) & (k <= r + ahead), s[STACK * g : STACK * (g + 1), BLK:], NEG))
            scores.append(jnp.concatenate([s[:, :BLK], jnp.concatenate(last, axis=0)], axis=1))
        maxima = [jnp.max(s, axis=1, keepdims=True) * C2 for s in scores]
        weights = [jnp.exp2(s * C2 - m).astype(BF16) for s, m in zip(scores, maxima)]
        results = [dot(p, vall[b]) for p, (_, b, _) in zip(weights, pairs)]
        for (_, _, rows), m, o in zip(pairs, maxima, results):
            old = pm[rows]
            top = jnp.maximum(old, m)
            f_old, f = jnp.exp2(old - top), jnp.exp2(m - top)
            pm[rows] = top
            po[rows, :HEAD] = po[rows, :HEAD] * f_old + o[:, :HEAD] * f
            po[rows, HEAD:] = po[rows, HEAD:] * f_old + o[:, HEAD:] * f

        @pl.when(i >= 2)
        def _():
            for g in range(QUAD):
                send_partial((i - 2) * QUAD + g)

        return carry

    lane = lax.broadcasted_iota(jnp.int32, (ROWS, 128), 1)

    def r3_send(j):
        return remote(r3s.at[j], r3d.at[j], r3_ss.at[j], r3_rr.at[j], at_z(2 + j))

    def send_partial(j):
        stats = jnp.zeros((ROWS, 128), F32)
        for h in range(HEADS):
            rows = pl.ds(pl.multiple_of((j * HEADS + h) * ROWS, ROWS), ROWS)
            m = pm[rows]
            even = jnp.ceil(m * 0.25) * 4
            f = jnp.exp2(m - even)
            r3s[j, :, HEAD * h : HEAD * (h + 1)] = (po[rows, :HEAD] * f).astype(BF16)
            total = po[rows, HEAD:] * f
            high = total.astype(BF16).astype(F32)
            stats = jnp.where(lane == h, high, stats)
            stats = jnp.where(lane == 8 + h, total - high, stats)
            stats = jnp.where(lane == 16 + h, even, stats)
        r3s[j, :, WIDE:] = stats.astype(BF16)

        @pl.when(j != 6)
        def _():
            r3_send(j).start()

    lax.fori_loop(0, 4, prompt, 0)
    anchor_along_y()
    lax.fori_loop(EARLY, HEADS // 2, loop_a, 0)

    seen = jnp.where(c > 0, 0.0, NEG)

    def anchor_unit(h, carry):
        cols = pl.ds(pl.multiple_of(h * HEAD, HEAD), HEAD)
        s = dot(q_v[:, cols], kta[...])
        m = jnp.max(s, axis=1, keepdims=True)
        o = dot(jnp.exp2(s * C2 - m * C2).astype(BF16), vaa[...])
        m = m + seen
        own = om[h, :, 2 * HEAD :]
        top = jnp.maximum(m, own)
        f_own, f = jnp.exp2((own - top) * C2), jnp.exp2((m - top) * C2)
        above = om[h, :, :HEAD] * f_own + o[:, :HEAD] * f
        below = om[h, :, HEAD : 2 * HEAD] * f_own + o[:, HEAD:] * f
        out_v[:, cols] = (above / below).astype(BF16)
        return carry

    for j in range(NZ):
        if j != 6:
            arrived(r3d.at[j], r3_rr.at[j])
    parts = [r3s if j == 6 else r3d for j in range(NZ)]
    stats = [parts[j][j, :, WIDE:].astype(F32) for j in range(NZ)]
    top = functools.reduce(jnp.maximum, stats)
    factors = [jnp.exp2(s - top) for s in stats]
    total = sum(
        (s + pltpu.roll(s, 120, 1)) * pltpu.roll(f, 112, 1) for s, f in zip(stats, factors)
    )
    for h in range(HEADS):
        cols = slice(HEAD * h, HEAD * (h + 1))
        merged = sum(
            parts[j][j, :, cols].astype(F32) * factors[j][:, 16 + h : 17 + h] for j in range(NZ)
        )
        att[z, :, cols] = (merged / total[:, h : h + 1]).astype(BF16)

    def a_send(d):
        return remote(att.at[z], att.at[z], a_ss.at[d], a_rr.at[z], at_z(d))

    for d in FAR_FIRST:
        a_send(d).start()

    w_wait(0, down)
    w_send(0, down, up, 2).start()
    w_wait(1, up)
    w_send(1, up, down, 2).start()

    for row in (up, down, far):
        arrived(anc.at[row], n_yr.at[row])
    for i in range(NY):
        at = slice(PIECE * i, PIECE * (i + 1))
        kta[:, at] = jnp.concatenate([anc[i, p] for p in range(NZ // 2)], axis=0).T
        vaa[at, :HEAD] = jnp.concatenate([anc[i, NZ // 2 + p] for p in range(NZ // 2)], axis=0)

    lax.fori_loop(0, AG_UNITS, anchor_unit, 0)
    enc_out = [
        pltpu.make_async_copy(out_v.at[:, cols], enc.at[:, cols], loc.at[8 + i])
        for i, cols in enumerate((pl.ds(0, AG_UNITS * HEAD), pl.ds(AG_UNITS * HEAD, (HEADS - AG_UNITS) * HEAD)))
    ]
    enc_out[0].start()

    for part in range(2):
        if part == 0:
            w_wait(0, up)
            w_wait(1, down)
        w_wait(part, far)
    for d in range(1, NZ):
        arrived(att.at[(z + d) % NZ], a_rr.at[(z + d) % NZ])
    rows = jnp.concatenate([att[i] for i in range(NZ)], axis=0)
    for b in range(NY):
        part = dot(rows, wall[b])
        for i in range(2):
            pacc[i, :, FEATS * b : FEATS * (b + 1)] = part[HALF * i : HALF * (i + 1)]

    c_send = remote(pacc.at[1 - core], pgot, c_ss, c_rr, (c, x * NK + 1 - core))
    c_send.start()
    c_send.wait_recv()

    def f_send(row):
        return remote(fsend.at[row], fgot.at[x], f_ss.at[row], f_rr.at[x], (row * NZ + z, y * NK + core))

    for row in range(NY):
        cols = slice(FEATS * row, FEATS * (row + 1))
        piece = pacc[core, :, cols] + pgot[:, cols]
        home = (x == y) & (y == row)

        @pl.when(home)
        def _(piece=piece):
            fgot[x] = piece.astype(BF16)

        @pl.when(jnp.logical_not(home))
        def _(piece=piece, row=row):
            fsend[row] = piece.astype(BF16)
            f_send(row).start()

    lax.fori_loop(AG_UNITS, HEADS, anchor_unit, 0)
    enc_out[1].start()

    for other in range(NX):
        @pl.when((other != x) | (x != y))
        def _(other=other):
            arrived(fgot.at[other], f_rr.at[other])
    ans[...] = sum(fgot[i].astype(F32) for i in range(NX)).astype(BF16)

    for d in range(1, NZ):
        q_send(d).wait_send()
        anchor_z(d).wait_send()
        a_send(d).wait_send()

    @pl.when(c == 0)
    def _():
        for p in range(1, NZ):
            root_send(p).wait_send()

    @pl.when(y == 0)
    def _():
        for row in (2, 1, 3):
            quarter_send(row).wait_send()

    for i, row in enumerate((far, up, down)):
        anchor_y(row, i).wait_send()

    for i, row in enumerate((y, y, down)):
        k_send(row, up, i).wait_send()
        w_send(0, row, up, i).wait_send()
        w_send(1, row, up, i).wait_send()
        v_send(row, up, i).wait_send()
    for j in range(NZ):
        if j != 6:
            r3_send(j).wait_send()
    c_send.wait_send()
    for row in range(NY):
        @pl.when((x != y) | (y != row))
        def _(row=row):
            f_send(row).wait_send()
    for copy in enc_out:
        copy.wait()


PARTS = 4


def publish(enc, ans, enc_out, ans_out, held, held_ans, into, out):
    tall = BLK // PARTS
    pairs = [(ans, held_ans, ans_out)]
    for i in range(PARTS):
        rows = pl.ds(tall * i, tall)
        pairs.append((enc.at[rows], held.at[rows], enc_out.at[rows]))
    reads = [pltpu.make_async_copy(src, mid, into.at[i]) for i, (src, mid, _) in enumerate(pairs)]
    writes = [pltpu.make_async_copy(mid, dst, out.at[i]) for i, (_, mid, dst) in enumerate(pairs)]
    for copy in reads:
        copy.start()
    for read, write in zip(reads, writes):
        read.wait()
        write.start()
    for copy in writes:
        copy.wait()


def on_device(cq, ck, cv, pq, pk, pv, w):
    vm, dma = pltpu.VMEM, pltpu.SemaphoreType.DMA
    any_space = pl.BlockSpec(memory_space=pl.ANY)
    results = pl.pallas_call(
        kernel,
        out_shape=(
            jax.ShapeDtypeStruct((BLK, WIDE), BF16),
            jax.ShapeDtypeStruct((HALF, FEATS), BF16),
        ),
        in_specs=[any_space] * 7,
        out_specs=(any_space, pl.BlockSpec(memory_space=pltpu.VMEM)),
        scratch_shapes=[
            vm((BLK, WIDE), BF16), vm((NY, KEYS, HEAD), BF16), vm((NY, HELD, HEAD), BF16), vm((NY, KEYS, 2 * HEAD), BF16),
            vm((NY, WIDE, FEATS), BF16), vm((NY, HEAD, KEYS), BF16),
            vm((HEAD, BLK), BF16), vm((BLK, 2 * HEAD), BF16),
            vm((HEADS, BLK, 3 * HEAD), F32), vm((BLK, WIDE), BF16),
            vm((NZ, ROWS, WIDE), BF16), vm((NZ * HEADS * ROWS, HEAD), BF16),
            vm((NZ * HEADS * ROWS, 2 * HEAD), F32), vm((NZ * HEADS * ROWS, HEAD), F32),
            vm((NZ, ROWS, WIDE), BF16), vm((PIECE, HEAD), BF16), vm((NY, NZ, QUARTER, HEAD), BF16),
            vm((NZ, ROWS, MSG), BF16), vm((NZ, ROWS, MSG), BF16),
            vm((2, HALF, NY * FEATS), F32), vm((HALF, NY * FEATS), F32),
            vm((NY, HALF, FEATS), BF16), vm((NX, HALF, FEATS), BF16),
            dma((10,)), dma((NZ,)), dma((NZ,)), dma((3,)), dma((NY,)), dma((3,)), dma((NY,)),
            dma((2, 3)), dma((2, NY)),
            dma((NZ,)), dma((NY,)), dma((NZ,)), dma((3,)), dma((2,)), dma((NZ,)), dma((NY,)), dma((NZ,)), dma((NZ,)),
            dma((NZ,)), dma((NZ,)), dma, dma, dma((NY,)), dma((NX,)),
        ],
        compiler_params=pltpu.CompilerParams(
            collective_id=0, has_side_effects=True, vmem_limit_bytes=56 * 2**20
        ),
        cost_estimate=pl.CostEstimate(flops=12 * 10**9, bytes_accessed=5 * 10**6, transcendentals=11 * 10**6),
        name="star",
    )(cq, ck, cv, pq, pk, pv, w)
    return pl.pallas_call(
        publish,
        out_shape=tuple(jax.ShapeDtypeStruct(r.shape, r.dtype) for r in results),
        in_specs=[any_space] * 2,
        out_specs=(any_space,) * 2,
        scratch_shapes=[vm((BLK, WIDE), BF16), vm((HALF, FEATS), BF16), dma((PARTS + 1,)), dma((PARTS + 1,))],
        compiler_params=pltpu.CompilerParams(vmem_limit_bytes=56 * 2**20),
        name="publish",
    )(*results)


def solution(mesh):
    placed = (P("ctx", "tp"),) * 6 + (P("tp", "ctx"),)
    return jax.shard_map(
        on_device,
        mesh=mesh,
        in_specs=placed,
        out_specs=(P("ctx", "tp"), P("tp", "ctx")),
        check_vma=False,
    )
```

```python
import functools

import jax
import jax.numpy as jnp
from jax import lax
from jax.experimental import pallas as pl
from jax.experimental.pallas import tpu as pltpu
from jax.sharding import PartitionSpec as P

MESH = pl.DeviceIdType.MESH
F32 = jnp.float32
BF16 = jnp.bfloat16
HEAD = 128
HEADS = 8
NY, NZ, NX, NK = 4, 8, 4, 2
BLK = 768
ROWS = 16
WIDE = HEADS * HEAD
MSG = WIDE + 128
HELD = BLK + ROWS
KEYS = BLK + 128
PIECE = 2 * BLK // NZ
SHARE = PIECE // 2
EARLY = 3
AG_UNITS = 3
HALF = NZ * ROWS // 2
FEATS = 256
C2 = HEAD**-0.5 * 1.4426950408889634
NEG = -1e30
FAR_FIRST = (4, 3, 5, 2, 6, 1, 7)


def dot(a, b):
    return jnp.dot(a, b, preferred_element_type=F32)


def kernel(
    cq, ck, cv, pq, pk, pv, w,
    enc, ans,
    q_v, kall, vgot, vall, wall, kt, kta, vaa, om, out_v,
    qz, qst, po, pm, att, stage, anc, r3s, r3d,
    pacc, pgot, fsend, fgot,
    loc, q_ss, q_rr, k_ss, k_rr, v_ss, v_rr, w_ss, w_rr,
    n_ss, n_qs, n_zs, n_ys, n_rr, n_zr, n_yr, r3_ss, r3_rr, a_ss, a_rr, c_ss, c_rr, f_ss, f_rr,
):
    c = lax.axis_index("ctx")
    t = lax.axis_index("tp")
    y, z = c // NZ, c % NZ
    x, core = t // NK, t % NK
    up, down, far = (y + 1) % NY, (y + NY - 1) % NY, (y + 2) % NY

    def remote(src, dst, ss, rr, dev):
        return pltpu.make_async_remote_copy(
            src_ref=src, dst_ref=dst, send_sem=ss, recv_sem=rr,
            device_id=dev, device_id_type=MESH,
        )

    def arrived(ref, sem):
        pltpu.make_async_copy(ref, ref, sem).wait()

    def at_z(d):
        return (y * NZ + (z + d) % NZ, t)

    def at_y(row):
        return (row * NZ + z, t)

    local_q = pltpu.make_async_copy(pq, qz.at[z], loc.at[0])
    local_kv = [
        pltpu.make_async_copy(ck, kall.at[y, pl.ds(0, BLK)], loc.at[1]),
        pltpu.make_async_copy(pk, kall.at[y, pl.ds(BLK, ROWS)], loc.at[2]),
        pltpu.make_async_copy(cv, vgot.at[y, pl.ds(0, BLK)], loc.at[3]),
        pltpu.make_async_copy(pv, vgot.at[y, pl.ds(BLK, ROWS)], loc.at[4]),
    ]
    local_rest = [
        pltpu.make_async_copy(cq, q_v, loc.at[5]),
        pltpu.make_async_copy(w, wall.at[y], loc.at[6]),
    ]
    local_q.start()
    for copy in local_kv + local_rest:
        copy.start()

    barrier = pltpu.get_barrier_semaphore()

    def greet(dev):
        pl.semaphore_signal(barrier, inc=1, device_id=dev, device_id_type=MESH)

    for d in range(1, NZ):
        greet(at_z(d))
    greet(at_y(up))
    greet(at_y(down))
    greet(at_y(far))
    greet((c, x * NK + 1 - core))
    for other in range(NX):
        @pl.when((other != x) | (x != y))
        def _(other=other):
            greet((x * NZ + z, other * NK + core))
    pl.semaphore_wait(barrier, NZ - 1 + 3 + 1 + NY - jnp.where(x == y, 1, 0))

    def q_send(d):
        return remote(qz.at[z], qz.at[z], q_ss.at[d], q_rr.at[z], at_z(d))


    half_of = y % 2
    partner = y + 1 - 2 * half_of

    def root_send(p):
        if p < NZ // 2:
            src = ck.at[pl.ds(p * PIECE, PIECE)]
        else:
            src = cv.at[pl.ds((p - NZ // 2) * PIECE, PIECE)]
        return remote(src, stage, n_ss.at[p], n_rr.at[0], (p, t))

    def share_send(row):
        src = stage.at[pl.ds(row % 2 * SHARE, SHARE)]
        return remote(src, anc.at[row % 2, z], n_qs.at[row], n_rr.at[1], at_y(row))

    def anchor_z(d):
        return remote(anc.at[half_of, z], anc.at[half_of, z], n_zs.at[d], n_zr.at[z], at_z(d))

    anchor_y = remote(anc.at[half_of], anc.at[half_of], n_ys, n_yr, at_y(partner))

    root_own = pltpu.make_async_copy(ck.at[pl.ds(0, PIECE)], stage, loc.at[7])

    @pl.when(c == 0)
    def _():
        root_own.start()
        for p in FAR_FIRST:
            root_send(p).start()

    local_q.wait()
    for d in FAR_FIRST:
        q_send(d).start()

    def anchor_shares():
        @pl.when(c == 0)
        def _():
            root_own.wait()

        @pl.when(c != 0)
        def _():
            arrived(stage, n_rr.at[0])

        for row in (2, 1, 3):
            share_send(row).start()
        anc[0, z] = stage[:SHARE]
        for d in FAR_FIRST:
            anchor_z(d).start()

    def anchor_along_z():
        arrived(anc.at[half_of, z], n_rr.at[1])
        for d in FAR_FIRST:
            anchor_z(d).start()

    def anchor_along_y():
        for d in range(1, NZ):
            arrived(anc.at[half_of, (z + d) % NZ], n_zr.at[(z + d) % NZ])
        anchor_y.start()

    def keys_of(row):
        return kall.at[row, pl.ds(0, HELD)]

    def values_of(row):
        return vgot.at[row]

    def spread_values(row):
        vall[row, :HELD, :HEAD] = vgot[row]

    def k_send(row, to, i):
        return remote(keys_of(row), keys_of(row), k_ss.at[i], k_rr.at[row], at_y(to))

    def v_send(row, to, i):
        return remote(values_of(row), values_of(row), v_ss.at[i], v_rr.at[row], at_y(to))

    for copy in local_kv:
        copy.wait()
    k_send(y, up, 0).start()
    v_send(y, down, 1).start()
    v_send(y, up, 0).start()
    k_send(y, down, 1).start()

    W_ROWS = WIDE // 2

    def w_send(part, row, to, i):
        ref = wall.at[row, pl.ds(part * W_ROWS, W_ROWS)]
        return remote(ref, ref, w_ss.at[part, i], w_rr.at[part, row], at_y(to))

    def w_wait(part, row):
        arrived(wall.at[row, pl.ds(part * W_ROWS, W_ROWS)], w_rr.at[part, row])

    for b in range(NY):
        kall[b, HELD:] = jnp.zeros((KEYS - HELD, HEAD), BF16)
        vall[b, HELD:, :HEAD] = jnp.zeros((KEYS - HELD, HEAD), BF16)
        vall[b, :, HEAD:] = jnp.ones((KEYS, HEAD), BF16)
    vaa[:, HEAD:] = jnp.ones((BLK, HEAD), BF16)
    po[...] = jnp.zeros(po.shape, F32)
    pm[...] = jnp.full(pm.shape, NEG, F32)
    kt[y] = kall[y].T
    spread_values(y)
    for copy in local_rest:
        copy.wait()

    def own_head(h):
        cols = pl.ds(pl.multiple_of(h * HEAD, HEAD), HEAD)
        r = 256
        row = lax.broadcasted_iota(jnp.int32, (r, r), 0)
        col = lax.broadcasted_iota(jnp.int32, (r, r), 1)
        tiles = range(BLK // r)
        scores = []
        for i in tiles:
            s = dot(q_v[r * i : r * (i + 1), cols], kt[y, :, : r * (i + 1)])
            last = jnp.where(col <= row, s[:, r * i :], NEG)
            scores.append(jnp.concatenate([s[:, : r * i], last], axis=1) if i else last)
        maxima = [jnp.max(s, axis=1, keepdims=True) for s in scores]
        weights = [jnp.exp2(s * C2 - m * C2).astype(BF16) for s, m in zip(scores, maxima)]
        for i in tiles:
            om[h, r * i : r * (i + 1), : 2 * HEAD] = dot(weights[i], vall[y, : r * (i + 1)])
            om[h, r * i : r * (i + 1), 2 * HEAD :] = jnp.broadcast_to(maxima[i], (r, HEAD))

    def loop_a(j, carry):
        own_head(2 * j)
        own_head(2 * j + 1)

        return carry

    lax.fori_loop(0, EARLY, loop_a, 0)
    arrived(keys_of(down), k_rr.at[down])
    k_send(down, up, 2).start()
    arrived(values_of(up), v_rr.at[up])
    v_send(up, down, 2).start()

    @pl.when(y == 0)
    def _():
        anchor_shares()

    w_send(0, y, up, 0).start()
    w_send(1, y, down, 1).start()
    w_send(1, y, up, 0).start()
    w_send(0, y, down, 1).start()

    def turn(j):
        return (z + 2 + j) % NZ

    for d in range(1, NZ):
        arrived(qz.at[(z + d) % NZ], q_rr.at[(z + d) % NZ])
    for j in range(NZ):
        for h in range(HEADS):
            qst[(j * HEADS + h) * ROWS : (j * HEADS + h + 1) * ROWS] = qz[turn(j), :, HEAD * h : HEAD * (h + 1)]
    kt[down] = kall[down].T

    QUAD = 4
    STACK = HEADS * ROWS

    def prompt(i, carry):
        halves = (0, 1)
        steps = (jnp.where(i == 0, 0, jnp.where(i == 1, 3, i - 1)),) * 2

        @pl.when(i == 1)
        def _():
            arrived(values_of(down), v_rr.at[down])
            spread_values(down)

        @pl.when(i == 2)
        def _():
            arrived(keys_of(up), k_rr.at[up])
            kt[up] = kall[up].T
            spread_values(up)

        @pl.when(i == 3)
        def _():
            arrived(keys_of(far), k_rr.at[far])
            arrived(values_of(far), v_rr.at[far])
            kt[far] = kall[far].T
            spread_values(far)

        @pl.when((i == 3) & (y != 0))
        def _():
            anchor_along_z()

        r = lax.broadcasted_iota(jnp.int32, (STACK, 128), 0) % ROWS
        k = lax.broadcasted_iota(jnp.int32, (STACK, 128), 1)
        pairs = [
            (a, (y + step) % NY, pl.ds(a * (QUAD * STACK), QUAD * STACK))
            for a, step in zip(halves, steps)
        ]
        scores = []
        for a, b, rows in pairs:
            s = dot(qst[rows], kt[b])
            last = []
            for g in range(QUAD):
                ahead = (y * NZ + turn(a * QUAD + g) - (b * NZ + z)) * ROWS
                last.append(jnp.where((k < ROWS) & (k <= r + ahead), s[STACK * g : STACK * (g + 1), BLK:], NEG))
            scores.append(jnp.concatenate([s[:, :BLK], jnp.concatenate(last, axis=0)], axis=1))
        maxima = [jnp.max(s, axis=1, keepdims=True) * C2 for s in scores]
        weights = [jnp.exp2(s * C2 - m).astype(BF16) for s, m in zip(scores, maxima)]
        results = [dot(p, vall[b]) for p, (_, b, _) in zip(weights, pairs)]
        for (_, _, rows), m, o in zip(pairs, maxima, results):
            old = pm[rows]
            top = jnp.maximum(old, m)
            f_old, f = jnp.exp2(old - top), jnp.exp2(m - top)
            pm[rows] = top
            po[rows, :HEAD] = po[rows, :HEAD] * f_old + o[:, :HEAD] * f
            po[rows, HEAD:] = po[rows, HEAD:] * f_old + o[:, HEAD:] * f

        return carry

    lane = lax.broadcasted_iota(jnp.int32, (ROWS, 128), 1)

    def r3_send(j):
        return remote(r3s.at[j], r3d.at[j], r3_ss.at[j], r3_rr.at[j], at_z(2 + j))

    def send_partial(j):
        stats = jnp.zeros((ROWS, 128), F32)
        for h in range(HEADS):
            rows = slice((j * HEADS + h) * ROWS, (j * HEADS + h + 1) * ROWS)
            m = pm[rows]
            even = jnp.ceil(m * 0.25) * 4
            f = jnp.exp2(m - even)
            r3s[j, :, HEAD * h : HEAD * (h + 1)] = (po[rows, :HEAD] * f).astype(BF16)
            total = po[rows, HEAD:] * f
            high = total.astype(BF16).astype(F32)
            stats = jnp.where(lane == h, high, stats)
            stats = jnp.where(lane == 8 + h, total - high, stats)
            stats = jnp.where(lane == 16 + h, even, stats)
        r3s[j, :, WIDE:] = stats.astype(BF16)

        if j != 6:
            r3_send(j).start()

    lax.fori_loop(0, NY, prompt, 0)
    for j in (2, 1, 3, 0, 4, 7, 5, 6):
        send_partial(j)
    lax.fori_loop(EARLY, HEADS // 2, loop_a, 0)
    anchor_along_y()

    seen = jnp.where(c > 0, 0.0, NEG)

    def anchor_unit(h, carry):
        cols = pl.ds(pl.multiple_of(h * HEAD, HEAD), HEAD)
        s = dot(q_v[:, cols], kta[...])
        m = jnp.max(s, axis=1, keepdims=True)
        o = dot(jnp.exp2(s * C2 - m * C2).astype(BF16), vaa[...])
        m = m + seen
        own = om[h, :, 2 * HEAD :]
        top = jnp.maximum(m, own)
        f_own, f = jnp.exp2((own - top) * C2), jnp.exp2((m - top) * C2)
        above = om[h, :, :HEAD] * f_own + o[:, :HEAD] * f
        below = om[h, :, HEAD : 2 * HEAD] * f_own + o[:, HEAD:] * f
        out_v[:, cols] = (above / below).astype(BF16)
        return carry

    w_wait(0, down)
    w_send(0, down, up, 2).start()
    w_wait(1, up)
    w_send(1, up, down, 2).start()

    for j in range(NZ):
        if j != 6:
            arrived(r3d.at[j], r3_rr.at[j])
    parts = [r3s if j == 6 else r3d for j in range(NZ)]
    stats = [parts[j][j, :, WIDE:].astype(F32) for j in range(NZ)]
    top = functools.reduce(jnp.maximum, stats)
    factors = [jnp.exp2(s - top) for s in stats]
    total = sum(
        (s + pltpu.roll(s, 120, 1)) * pltpu.roll(f, 112, 1) for s, f in zip(stats, factors)
    )
    for h in range(HEADS):
        cols = slice(HEAD * h, HEAD * (h + 1))
        merged = sum(
            parts[j][j, :, cols].astype(F32) * factors[j][:, 16 + h : 17 + h] for j in range(NZ)
        )
        att[z, :, cols] = (merged / total[:, h : h + 1]).astype(BF16)

    def a_send(d):
        return remote(att.at[z], att.at[z], a_ss.at[d], a_rr.at[z], at_z(d))

    for d in FAR_FIRST:
        a_send(d).start()

    arrived(anc.at[1 - half_of], n_yr)
    for i in range(2):
        at = slice(BLK // 2 * i, BLK // 2 * (i + 1))
        kta[:, at] = jnp.concatenate([anc[i, p] for p in range(NZ // 2)], axis=0).T
        vaa[at, :HEAD] = jnp.concatenate([anc[i, NZ // 2 + p] for p in range(NZ // 2)], axis=0)

    lax.fori_loop(0, AG_UNITS, anchor_unit, 0)
    enc_out = [
        pltpu.make_async_copy(out_v.at[:, cols], enc.at[:, cols], loc.at[8 + i])
        for i, cols in enumerate((pl.ds(0, AG_UNITS * HEAD), pl.ds(AG_UNITS * HEAD, (HEADS - AG_UNITS) * HEAD)))
    ]
    enc_out[0].start()

    for part in range(2):
        if part == 0:
            w_wait(0, up)
            w_wait(1, down)
        w_wait(part, far)
    for d in range(1, NZ):
        arrived(att.at[(z + d) % NZ], a_rr.at[(z + d) % NZ])
    rows = jnp.concatenate([att[i] for i in range(NZ)], axis=0)
    for b in range(NY):
        part = dot(rows, wall[b])
        for i in range(2):
            pacc[i, :, FEATS * b : FEATS * (b + 1)] = part[HALF * i : HALF * (i + 1)]

    c_send = remote(pacc.at[1 - core], pgot, c_ss, c_rr, (c, x * NK + 1 - core))
    c_send.start()
    c_send.wait_recv()

    def f_send(row):
        return remote(fsend.at[row], fgot.at[x], f_ss.at[row], f_rr.at[x], (row * NZ + z, y * NK + core))

    for row in range(NY):
        cols = slice(FEATS * row, FEATS * (row + 1))
        piece = pacc[core, :, cols] + pgot[:, cols]
        home = (x == y) & (y == row)

        @pl.when(home)
        def _(piece=piece):
            fgot[x] = piece.astype(BF16)

        @pl.when(jnp.logical_not(home))
        def _(piece=piece, row=row):
            fsend[row] = piece.astype(BF16)
            f_send(row).start()

    lax.fori_loop(AG_UNITS, HEADS, anchor_unit, 0)
    enc_out[1].start()

    for other in range(NX):
        @pl.when((other != x) | (x != y))
        def _(other=other):
            arrived(fgot.at[other], f_rr.at[other])
    ans[...] = sum(fgot[i].astype(F32) for i in range(NX)).astype(BF16)

    for d in range(1, NZ):
        q_send(d).wait_send()
        anchor_z(d).wait_send()
        a_send(d).wait_send()

    @pl.when(c == 0)
    def _():
        for p in range(1, NZ):
            root_send(p).wait_send()

    @pl.when(y == 0)
    def _():
        for row in (2, 1, 3):
            share_send(row).wait_send()

    anchor_y.wait_send()

    for i, row in enumerate((y, y, down)):
        k_send(row, up, i).wait_send()
        w_send(0, row, up, i).wait_send()
        w_send(1, row, up, i).wait_send()
        v_send(row, up, i).wait_send()
    for j in range(NZ):
        if j != 6:
            r3_send(j).wait_send()
    c_send.wait_send()
    for row in range(NY):
        @pl.when((x != y) | (y != row))
        def _(row=row):
            f_send(row).wait_send()
    for copy in enc_out:
        copy.wait()


PARTS = 4


def publish(enc, ans, enc_out, ans_out, held, held_ans, into, out):
    tall = BLK // PARTS
    pairs = [(ans, held_ans, ans_out)]
    for i in range(PARTS):
        rows = pl.ds(tall * i, tall)
        pairs.append((enc.at[rows], held.at[rows], enc_out.at[rows]))
    reads = [pltpu.make_async_copy(src, mid, into.at[i]) for i, (src, mid, _) in enumerate(pairs)]
    writes = [pltpu.make_async_copy(mid, dst, out.at[i]) for i, (_, mid, dst) in enumerate(pairs)]
    for copy in reads:
        copy.start()
    for read, write in zip(reads, writes):
        read.wait()
        write.start()
    for copy in writes:
        copy.wait()


def on_device(cq, ck, cv, pq, pk, pv, w):
    vm, dma = pltpu.VMEM, pltpu.SemaphoreType.DMA
    any_space = pl.BlockSpec(memory_space=pl.ANY)
    results = pl.pallas_call(
        kernel,
        out_shape=(
            jax.ShapeDtypeStruct((BLK, WIDE), BF16),
            jax.ShapeDtypeStruct((HALF, FEATS), BF16),
        ),
        in_specs=[any_space] * 7,
        out_specs=(any_space, pl.BlockSpec(memory_space=pltpu.VMEM)),
        scratch_shapes=[
            vm((BLK, WIDE), BF16), vm((NY, KEYS, HEAD), BF16), vm((NY, HELD, HEAD), BF16), vm((NY, KEYS, 2 * HEAD), BF16),
            vm((NY, WIDE, FEATS), BF16), vm((NY, HEAD, KEYS), BF16),
            vm((HEAD, BLK), BF16), vm((BLK, 2 * HEAD), BF16),
            vm((HEADS, BLK, 3 * HEAD), F32), vm((BLK, WIDE), BF16),
            vm((NZ, ROWS, WIDE), BF16), vm((NZ * HEADS * ROWS, HEAD), BF16),
            vm((NZ * HEADS * ROWS, 2 * HEAD), F32), vm((NZ * HEADS * ROWS, HEAD), F32),
            vm((NZ, ROWS, WIDE), BF16), vm((PIECE, HEAD), BF16), vm((2, NZ, SHARE, HEAD), BF16),
            vm((NZ, ROWS, MSG), BF16), vm((NZ, ROWS, MSG), BF16),
            vm((2, HALF, NY * FEATS), F32), vm((HALF, NY * FEATS), F32),
            vm((NY, HALF, FEATS), BF16), vm((NX, HALF, FEATS), BF16),
            dma((10,)), dma((NZ,)), dma((NZ,)), dma((3,)), dma((NY,)), dma((3,)), dma((NY,)),
            dma((2, 3)), dma((2, NY)),
            dma((NZ,)), dma((NY,)), dma((NZ,)), dma, dma((2,)), dma((NZ,)), dma, dma((NZ,)), dma((NZ,)),
            dma((NZ,)), dma((NZ,)), dma, dma, dma((NY,)), dma((NX,)),
        ],
        compiler_params=pltpu.CompilerParams(
            collective_id=0, has_side_effects=True, vmem_limit_bytes=56 * 2**20
        ),
        cost_estimate=pl.CostEstimate(flops=12 * 10**9, bytes_accessed=5 * 10**6, transcendentals=11 * 10**6),
        name="star",
    )(cq, ck, cv, pq, pk, pv, w)
    return pl.pallas_call(
        publish,
        out_shape=tuple(jax.ShapeDtypeStruct(r.shape, r.dtype) for r in results),
        in_specs=[any_space] * 2,
        out_specs=(any_space,) * 2,
        scratch_shapes=[vm((BLK, WIDE), BF16), vm((HALF, FEATS), BF16), dma((PARTS + 1,)), dma((PARTS + 1,))],
        compiler_params=pltpu.CompilerParams(vmem_limit_bytes=56 * 2**20),
        name="publish",
    )(*results)


def solution(mesh):
    placed = (P("ctx", "tp"),) * 6 + (P("tp", "ctx"),)
    return jax.shard_map(
        on_device,
        mesh=mesh,
        in_specs=placed,
        out_specs=(P("ctx", "tp"), P("tp", "ctx")),
        check_vma=False,
    )
```

```python
import functools

import jax
import jax.numpy as jnp
from jax import lax
from jax.experimental import pallas as pl
from jax.experimental.pallas import tpu as pltpu
from jax.sharding import PartitionSpec as P

MESH = pl.DeviceIdType.MESH
F32 = jnp.float32
BF16 = jnp.bfloat16
HEAD = 128
HEADS = 8
NY, NZ, NX, NK = 4, 8, 4, 2
BLK = 768
ROWS = 16
WIDE = HEADS * HEAD
MSG = WIDE + 128
HELD = BLK + ROWS
KEYS = BLK + 128
PIECE = 2 * BLK // NZ
SHARE = PIECE // 2
EARLY = 3
AG_UNITS = 3
HALF = NZ * ROWS // 2
FEATS = 256
C2 = HEAD**-0.5 * 1.4426950408889634
NEG = -1e30
FAR_FIRST = (4, 3, 5, 2, 6, 1, 7)


def dot(a, b):
    return jnp.dot(a, b, preferred_element_type=F32)


def kernel(
    cq, ck, cv, pq, pk, pv, w,
    enc, ans,
    q_v, kall, vgot, vall, wall, kt, kta, vaa, om, out_v,
    qz, qst, po, pm, att, stage, anc, r3s, r3d,
    pacc, pgot, fsend, fgot,
    loc, q_ss, q_rr, k_ss, k_rr, v_ss, v_rr, w_ss, w_rr,
    n_ss, n_qs, n_zs, n_ys, n_rr, n_zr, n_yr, r3_ss, r3_rr, a_ss, a_rr, c_ss, c_rr, f_ss, f_rr,
):
    c = lax.axis_index("ctx")
    t = lax.axis_index("tp")
    y, z = c // NZ, c % NZ
    x, core = t // NK, t % NK
    up, down, far = (y + 1) % NY, (y + NY - 1) % NY, (y + 2) % NY

    def remote(src, dst, ss, rr, dev):
        return pltpu.make_async_remote_copy(
            src_ref=src, dst_ref=dst, send_sem=ss, recv_sem=rr,
            device_id=dev, device_id_type=MESH,
        )

    def arrived(ref, sem):
        pltpu.make_async_copy(ref, ref, sem).wait()

    def at_z(d):
        return (y * NZ + (z + d) % NZ, t)

    def at_y(row):
        return (row * NZ + z, t)

    local_q = pltpu.make_async_copy(pq, qz.at[z], loc.at[0])
    local_kv = [
        pltpu.make_async_copy(ck, kall.at[y, pl.ds(0, BLK)], loc.at[1]),
        pltpu.make_async_copy(pk, kall.at[y, pl.ds(BLK, ROWS)], loc.at[2]),
        pltpu.make_async_copy(cv, vgot.at[y, pl.ds(0, BLK)], loc.at[3]),
        pltpu.make_async_copy(pv, vgot.at[y, pl.ds(BLK, ROWS)], loc.at[4]),
    ]
    local_rest = [
        pltpu.make_async_copy(cq, q_v, loc.at[5]),
        pltpu.make_async_copy(w, wall.at[y], loc.at[6]),
    ]
    local_q.start()
    for copy in local_kv + local_rest:
        copy.start()

    barrier = pltpu.get_barrier_semaphore()

    def greet(dev):
        pl.semaphore_signal(barrier, inc=1, device_id=dev, device_id_type=MESH)

    for d in range(1, NZ):
        greet(at_z(d))
    greet(at_y(up))
    greet(at_y(down))
    greet(at_y(far))
    greet((c, x * NK + 1 - core))
    for other in range(NX):
        @pl.when((other != x) | (x != y))
        def _(other=other):
            greet((x * NZ + z, other * NK + core))
    pl.semaphore_wait(barrier, NZ - 1 + 3 + 1 + NY - jnp.where(x == y, 1, 0))

    def q_send(d):
        return remote(qz.at[z], qz.at[z], q_ss.at[d], q_rr.at[z], at_z(d))


    half_of = y % 2
    partner = y + 1 - 2 * half_of

    def root_send(p):
        if p < NZ // 2:
            src = ck.at[pl.ds(p * PIECE, PIECE)]
        else:
            src = cv.at[pl.ds((p - NZ // 2) * PIECE, PIECE)]
        return remote(src, stage, n_ss.at[p], n_rr.at[0], (p, t))

    def share_send(row):
        src = stage.at[pl.ds(row % 2 * SHARE, SHARE)]
        return remote(src, anc.at[row % 2, z], n_qs.at[row], n_rr.at[1], at_y(row))

    def anchor_z(d):
        return remote(anc.at[half_of, z], anc.at[half_of, z], n_zs.at[d], n_zr.at[z], at_z(d))

    anchor_y = remote(anc.at[half_of], anc.at[half_of], n_ys, n_yr, at_y(partner))

    root_own = pltpu.make_async_copy(ck.at[pl.ds(0, PIECE)], stage, loc.at[7])

    @pl.when(c == 0)
    def _():
        root_own.start()
        for p in FAR_FIRST:
            root_send(p).start()

    local_q.wait()
    for d in FAR_FIRST:
        q_send(d).start()

    def anchor_shares():
        @pl.when(c == 0)
        def _():
            root_own.wait()

        @pl.when(c != 0)
        def _():
            arrived(stage, n_rr.at[0])

        for row in (2, 1, 3):
            share_send(row).start()
        anc[0, z] = stage[:SHARE]
        for d in FAR_FIRST:
            anchor_z(d).start()

    def anchor_along_z():
        arrived(anc.at[half_of, z], n_rr.at[1])
        for d in FAR_FIRST:
            anchor_z(d).start()

    def anchor_along_y():
        for d in range(1, NZ):
            arrived(anc.at[half_of, (z + d) % NZ], n_zr.at[(z + d) % NZ])
        anchor_y.start()

    def keys_of(row):
        return kall.at[row, pl.ds(0, HELD)]

    def values_of(row):
        return vgot.at[row]

    def spread_values(row):
        vall[row, :HELD, :HEAD] = vgot[row]

    def k_send(row, to, i):
        return remote(keys_of(row), keys_of(row), k_ss.at[i], k_rr.at[row], at_y(to))

    def v_send(row, to, i):
        return remote(values_of(row), values_of(row), v_ss.at[i], v_rr.at[row], at_y(to))

    for copy in local_kv:
        copy.wait()
    k_send(y, up, 0).start()
    v_send(y, down, 1).start()
    v_send(y, up, 0).start()
    k_send(y, down, 1).start()

    W_ROWS = WIDE // 2

    def w_send(part, row, to, i):
        ref = wall.at[row, pl.ds(part * W_ROWS, W_ROWS)]
        return remote(ref, ref, w_ss.at[part, i], w_rr.at[part, row], at_y(to))

    def w_wait(part, row):
        arrived(wall.at[row, pl.ds(part * W_ROWS, W_ROWS)], w_rr.at[part, row])

    for b in range(NY):
        kall[b, HELD:] = jnp.zeros((KEYS - HELD, HEAD), BF16)
        vall[b, HELD:, :HEAD] = jnp.zeros((KEYS - HELD, HEAD), BF16)
        vall[b, :, HEAD:] = jnp.ones((KEYS, HEAD), BF16)
    vaa[:, HEAD:] = jnp.ones((BLK, HEAD), BF16)
    po[...] = jnp.zeros(po.shape, F32)
    pm[...] = jnp.full(pm.shape, NEG, F32)
    kt[y] = kall[y].T
    spread_values(y)
    for copy in local_rest:
        copy.wait()

    def own_head(h):
        cols = pl.ds(pl.multiple_of(h * HEAD, HEAD), HEAD)
        r = 256
        row = lax.broadcasted_iota(jnp.int32, (r, r), 0)
        col = lax.broadcasted_iota(jnp.int32, (r, r), 1)
        tiles = range(BLK // r)
        scores = []
        for i in tiles:
            s = dot(q_v[r * i : r * (i + 1), cols], kt[y, :, : r * (i + 1)])
            last = jnp.where(col <= row, s[:, r * i :], NEG)
            scores.append(jnp.concatenate([s[:, : r * i], last], axis=1) if i else last)
        maxima = [jnp.max(s, axis=1, keepdims=True) for s in scores]
        weights = [jnp.exp2(s * C2 - m * C2).astype(BF16) for s, m in zip(scores, maxima)]
        for i in tiles:
            om[h, r * i : r * (i + 1), : 2 * HEAD] = dot(weights[i], vall[y, : r * (i + 1)])
            om[h, r * i : r * (i + 1), 2 * HEAD :] = jnp.broadcast_to(maxima[i], (r, HEAD))

    def loop_a(j, carry):
        own_head(2 * j)
        own_head(2 * j + 1)

        return carry

    lax.fori_loop(0, EARLY, loop_a, 0)
    arrived(keys_of(down), k_rr.at[down])
    k_send(down, up, 2).start()
    arrived(values_of(up), v_rr.at[up])
    v_send(up, down, 2).start()

    @pl.when(y == 0)
    def _():
        anchor_shares()

    w_send(0, y, up, 0).start()
    w_send(1, y, down, 1).start()
    w_send(1, y, up, 0).start()
    w_send(0, y, down, 1).start()

    def turn(j):
        return (z + 2 + j) % NZ

    for d in range(1, NZ):
        arrived(qz.at[(z + d) % NZ], q_rr.at[(z + d) % NZ])
    for j in range(NZ):
        for h in range(HEADS):
            qst[(j * HEADS + h) * ROWS : (j * HEADS + h + 1) * ROWS] = qz[turn(j), :, HEAD * h : HEAD * (h + 1)]
    kt[down] = kall[down].T

    QUAD = 4
    STACK = HEADS * ROWS

    def prompt(i, carry):
        halves = (0, 1)
        steps = (jnp.where(i == 0, 0, jnp.where(i == 1, 3, i - 1)),) * 2

        @pl.when(i == 1)
        def _():
            arrived(values_of(down), v_rr.at[down])
            spread_values(down)

        @pl.when(i == 2)
        def _():
            arrived(keys_of(up), k_rr.at[up])
            kt[up] = kall[up].T
            spread_values(up)

        @pl.when(i == 3)
        def _():
            arrived(keys_of(far), k_rr.at[far])
            arrived(values_of(far), v_rr.at[far])
            kt[far] = kall[far].T
            spread_values(far)

        @pl.when((i == 3) & (y != 0))
        def _():
            anchor_along_z()

        r = lax.broadcasted_iota(jnp.int32, (STACK, 128), 0) % ROWS
        k = lax.broadcasted_iota(jnp.int32, (STACK, 128), 1)
        pairs = [
            (a, (y + step) % NY, pl.ds(a * (QUAD * STACK), QUAD * STACK))
            for a, step in zip(halves, steps)
        ]
        scores = []
        for a, b, rows in pairs:
            s = dot(qst[rows], kt[b])
            last = []
            for g in range(QUAD):
                ahead = (y * NZ + turn(a * QUAD + g) - (b * NZ + z)) * ROWS
                last.append(jnp.where((k < ROWS) & (k <= r + ahead), s[STACK * g : STACK * (g + 1), BLK:], NEG))
            scores.append(jnp.concatenate([s[:, :BLK], jnp.concatenate(last, axis=0)], axis=1))
        maxima = [jnp.max(s, axis=1, keepdims=True) * C2 for s in scores]
        weights = [jnp.exp2(s * C2 - m).astype(BF16) for s, m in zip(scores, maxima)]
        results = [dot(p, vall[b]) for p, (_, b, _) in zip(weights, pairs)]
        for (_, _, rows), m, o in zip(pairs, maxima, results):
            old = pm[rows]
            top = jnp.maximum(old, m)
            f_old, f = jnp.exp2(old - top), jnp.exp2(m - top)
            pm[rows] = top
            po[rows, :HEAD] = po[rows, :HEAD] * f_old + o[:, :HEAD] * f
            po[rows, HEAD:] = po[rows, HEAD:] * f_old + o[:, HEAD:] * f

        return carry

    lane = lax.broadcasted_iota(jnp.int32, (ROWS, 128), 1)

    def r3_send(j):
        return remote(r3s.at[j], r3d.at[j], r3_ss.at[j], r3_rr.at[j], at_z(2 + j))

    def send_partial(j):
        stats = jnp.zeros((ROWS, 128), F32)
        for h in range(HEADS):
            rows = slice((j * HEADS + h) * ROWS, (j * HEADS + h + 1) * ROWS)
            m = pm[rows]
            even = jnp.ceil(m * 0.25) * 4
            f = jnp.exp2(m - even)
            r3s[j, :, HEAD * h : HEAD * (h + 1)] = (po[rows, :HEAD] * f).astype(BF16)
            total = po[rows, HEAD:] * f
            high = total.astype(BF16).astype(F32)
            stats = jnp.where(lane == h, high, stats)
            stats = jnp.where(lane == 8 + h, total - high, stats)
            stats = jnp.where(lane == 16 + h, even, stats)
        r3s[j, :, WIDE:] = stats.astype(BF16)

        if j != 6:
            r3_send(j).start()

    lax.fori_loop(0, NY, prompt, 0)
    for j in (2, 1, 3, 0, 4, 7, 5, 6):
        send_partial(j)
    lax.fori_loop(EARLY, HEADS // 2, loop_a, 0)
    anchor_along_y()

    seen = jnp.where(c > 0, 0.0, NEG)

    def anchor_unit(h, carry):
        cols = pl.ds(pl.multiple_of(h * HEAD, HEAD), HEAD)
        s = dot(q_v[:, cols], kta[...])
        m = jnp.max(s, axis=1, keepdims=True)
        o = dot(jnp.exp2(s * C2 - m * C2).astype(BF16), vaa[...])
        m = m + seen
        own = om[h, :, 2 * HEAD :]
        top = jnp.maximum(m, own)
        f_own, f = jnp.exp2((own - top) * C2), jnp.exp2((m - top) * C2)
        above = om[h, :, :HEAD] * f_own + o[:, :HEAD] * f
        below = om[h, :, HEAD : 2 * HEAD] * f_own + o[:, HEAD:] * f
        out_v[:, cols] = (above / below).astype(BF16)
        return carry

    w_wait(0, down)
    w_send(0, down, up, 2).start()
    w_wait(1, up)
    w_send(1, up, down, 2).start()

    for j in range(NZ):
        if j != 6:
            arrived(r3d.at[j], r3_rr.at[j])
    parts = [r3s if j == 6 else r3d for j in range(NZ)]
    stats = [parts[j][j, :, WIDE:].astype(F32) for j in range(NZ)]
    top = functools.reduce(jnp.maximum, stats)
    factors = [jnp.exp2(s - top) for s in stats]
    total = sum(
        (s + pltpu.roll(s, 120, 1)) * pltpu.roll(f, 112, 1) for s, f in zip(stats, factors)
    )
    for h in range(HEADS):
        cols = slice(HEAD * h, HEAD * (h + 1))
        merged = sum(
            parts[j][j, :, cols].astype(F32) * factors[j][:, 16 + h : 17 + h] for j in range(NZ)
        )
        att[z, :, cols] = (merged / total[:, h : h + 1]).astype(BF16)

    def a_send(d):
        return remote(att.at[z], att.at[z], a_ss.at[d], a_rr.at[z], at_z(d))

    for d in FAR_FIRST:
        a_send(d).start()

    arrived(anc.at[1 - half_of], n_yr)
    for i in range(2):
        at = slice(BLK // 2 * i, BLK // 2 * (i + 1))
        kta[:, at] = jnp.concatenate([anc[i, p] for p in range(NZ // 2)], axis=0).T
        vaa[at, :HEAD] = jnp.concatenate([anc[i, NZ // 2 + p] for p in range(NZ // 2)], axis=0)

    lax.fori_loop(0, AG_UNITS, anchor_unit, 0)
    enc_out = [
        pltpu.make_async_copy(out_v.at[:, cols], enc.at[:, cols], loc.at[8 + i])
        for i, cols in enumerate((pl.ds(0, AG_UNITS * HEAD), pl.ds(AG_UNITS * HEAD, (HEADS - AG_UNITS) * HEAD)))
    ]
    enc_out[0].start()

    w_wait(0, up)
    w_wait(1, down)
    for d in range(1, NZ):
        arrived(att.at[(z + d) % NZ], a_rr.at[(z + d) % NZ])
    rows = jnp.concatenate([att[i] for i in range(NZ)], axis=0)

    owners = (y, up, down, far)

    def c_send(i):
        return remote(pacc.at[1 - core, i], pgot.at[i], c_ss.at[i], c_rr.at[i], (c, x * NK + 1 - core))

    for i, row in enumerate(owners):
        if i == 3:
            w_wait(0, far)
            w_wait(1, far)
        part = dot(rows, wall[row])
        for half in range(2):
            pacc[half, i] = part[HALF * half : HALF * (half + 1)]
        c_send(i).start()

    def f_send(row):
        return remote(fsend.at[row], fgot.at[x], f_ss.at[row], f_rr.at[x], (row * NZ + z, y * NK + core))

    for i, row in enumerate(owners):
        c_send(i).wait_recv()
        piece = (pacc[core, i] + pgot[i]).astype(BF16)
        if i == 0:
            @pl.when(x == y)
            def _(piece=piece):
                fgot[x] = piece

            @pl.when(x != y)
            def _(piece=piece):
                fsend[y] = piece
                f_send(y).start()
        else:
            fsend[row] = piece
            f_send(row).start()

    lax.fori_loop(AG_UNITS, HEADS, anchor_unit, 0)
    enc_out[1].start()

    for other in range(NX):
        @pl.when((other != x) | (x != y))
        def _(other=other):
            arrived(fgot.at[other], f_rr.at[other])
    ans[...] = sum(fgot[i].astype(F32) for i in range(NX)).astype(BF16)

    for d in range(1, NZ):
        q_send(d).wait_send()
        anchor_z(d).wait_send()
        a_send(d).wait_send()

    @pl.when(c == 0)
    def _():
        for p in range(1, NZ):
            root_send(p).wait_send()

    @pl.when(y == 0)
    def _():
        for row in (2, 1, 3):
            share_send(row).wait_send()

    anchor_y.wait_send()

    for i, row in enumerate((y, y, down)):
        k_send(row, up, i).wait_send()
        w_send(0, row, up, i).wait_send()
        w_send(1, row, up, i).wait_send()
        v_send(row, up, i).wait_send()
    for j in range(NZ):
        if j != 6:
            r3_send(j).wait_send()
    for i in range(NY):
        c_send(i).wait_send()
    for row in range(NY):
        @pl.when((x != y) | (y != row))
        def _(row=row):
            f_send(row).wait_send()
    for copy in enc_out:
        copy.wait()


PARTS = 4


def publish(enc, ans, enc_out, ans_out, held, held_ans, into, out):
    tall = BLK // PARTS
    pairs = [(ans, held_ans, ans_out)]
    for i in range(PARTS):
        rows = pl.ds(tall * i, tall)
        pairs.append((enc.at[rows], held.at[rows], enc_out.at[rows]))
    reads = [pltpu.make_async_copy(src, mid, into.at[i]) for i, (src, mid, _) in enumerate(pairs)]
    writes = [pltpu.make_async_copy(mid, dst, out.at[i]) for i, (_, mid, dst) in enumerate(pairs)]
    for copy in reads:
        copy.start()
    for read, write in zip(reads, writes):
        read.wait()
        write.start()
    for copy in writes:
        copy.wait()


def on_device(cq, ck, cv, pq, pk, pv, w):
    vm, dma = pltpu.VMEM, pltpu.SemaphoreType.DMA
    any_space = pl.BlockSpec(memory_space=pl.ANY)
    results = pl.pallas_call(
        kernel,
        out_shape=(
            jax.ShapeDtypeStruct((BLK, WIDE), BF16),
            jax.ShapeDtypeStruct((HALF, FEATS), BF16),
        ),
        in_specs=[any_space] * 7,
        out_specs=(any_space, pl.BlockSpec(memory_space=pltpu.VMEM)),
        scratch_shapes=[
            vm((BLK, WIDE), BF16), vm((NY, KEYS, HEAD), BF16), vm((NY, HELD, HEAD), BF16), vm((NY, KEYS, 2 * HEAD), BF16),
            vm((NY, WIDE, FEATS), BF16), vm((NY, HEAD, KEYS), BF16),
            vm((HEAD, BLK), BF16), vm((BLK, 2 * HEAD), BF16),
            vm((HEADS, BLK, 3 * HEAD), F32), vm((BLK, WIDE), BF16),
            vm((NZ, ROWS, WIDE), BF16), vm((NZ * HEADS * ROWS, HEAD), BF16),
            vm((NZ * HEADS * ROWS, 2 * HEAD), F32), vm((NZ * HEADS * ROWS, HEAD), F32),
            vm((NZ, ROWS, WIDE), BF16), vm((PIECE, HEAD), BF16), vm((2, NZ, SHARE, HEAD), BF16),
            vm((NZ, ROWS, MSG), BF16), vm((NZ, ROWS, MSG), BF16),
            vm((2, NY, HALF, FEATS), F32), vm((NY, HALF, FEATS), F32),
            vm((NY, HALF, FEATS), BF16), vm((NX, HALF, FEATS), BF16),
            dma((10,)), dma((NZ,)), dma((NZ,)), dma((3,)), dma((NY,)), dma((3,)), dma((NY,)),
            dma((2, 3)), dma((2, NY)),
            dma((NZ,)), dma((NY,)), dma((NZ,)), dma, dma((2,)), dma((NZ,)), dma, dma((NZ,)), dma((NZ,)),
            dma((NZ,)), dma((NZ,)), dma((NY,)), dma((NY,)), dma((NY,)), dma((NX,)),
        ],
        compiler_params=pltpu.CompilerParams(
            collective_id=0, has_side_effects=True, vmem_limit_bytes=56 * 2**20
        ),
        cost_estimate=pl.CostEstimate(flops=12 * 10**9, bytes_accessed=5 * 10**6, transcendentals=11 * 10**6),
        name="star",
    )(cq, ck, cv, pq, pk, pv, w)
    return pl.pallas_call(
        publish,
        out_shape=tuple(jax.ShapeDtypeStruct(r.shape, r.dtype) for r in results),
        in_specs=[any_space] * 2,
        out_specs=(any_space,) * 2,
        scratch_shapes=[vm((BLK, WIDE), BF16), vm((HALF, FEATS), BF16), dma((PARTS + 1,)), dma((PARTS + 1,))],
        compiler_params=pltpu.CompilerParams(vmem_limit_bytes=56 * 2**20),
        name="publish",
    )(*results)


def solution(mesh):
    placed = (P("ctx", "tp"),) * 6 + (P("tp", "ctx"),)
    return jax.shard_map(
        on_device,
        mesh=mesh,
        in_specs=placed,
        out_specs=(P("ctx", "tp"), P("tp", "ctx")),
        check_vma=False,
    )
```
